128 devices in a mesh: row: 8 (over y, x_hi), col: 16 (over z, x_lo, core).
Axes of the slice: x: 4 (x_hi: 2, x_lo: 2; x = x_hi * 2 + x_lo), y: 4, z: 4, core: 2. Of those that a mesh axis runs over, the one named last changes fastest.
Arguments:
- alignment_embedding: bfloat16 [512, 768, 256], P(None, ('row', 'col')), may hold values from -6 to 6
- chosen_sequence_ids: int32 [128], replicated, may hold values from 0 to 511, as said below
- standardizer_scale: float32 [256], replicated, may hold values from 0.1 to 1.9
- standardizer_offset: float32 [256], replicated, may hold values from -3 to 3
- first_factor_matrix: bfloat16 [256, 32], replicated, may hold values from -0.375 to 0.375
- first_factor_shift: float32 [32], replicated, may hold values from -3 to 3
- second_factor_matrix: bfloat16 [256, 32], replicated, may hold values from -0.375 to 0.375
- second_factor_shift: float32 [32], replicated, may hold values from -3 to 3
- final_matrix: bfloat16 [1024, 128], replicated, may hold values from -0.1875 to 0.1875
- twosite_delta_cotangent: bfloat16 [768, 768, 128], P('row', 'col'), may hold values from -6 to 6
Outputs:
- chosen_sequence_slope: bfloat16 [128, 768, 256], P(None, ('row', 'col'))
- first_factor_matrix_slope: float32 [256, 32], replicated
- second_factor_matrix_slope: float32 [256, 32], replicated
- output_weight_gradient: float32 [1024, 128], replicated
The draws below stay inside these ranges and needn't reach their ends.
Inputs may be any that keep to these rules, and one draw needn't show every extreme that they name: `chosen_sequence_ids`: distinct row indices.
All inputs are finite; a program needn't handle non-finite values.
Results may differ from the reference program's by a relative error of at most 0.02.
Values may be sent and summed in bfloat16 or wider, within the bound.
A program may use at most 192 MiB of HBM per device.

```python
import jax
import jax.numpy as jnp
from jax import lax

CHANNEL_SPAN = 256
OUTER_FACTOR_DIM = 32
TWOSITE_CHANNELS = 128
ALIGNED_SEQS_ALL = 512
CHOSEN_SEQUENCES = 128
RES_DEV = 6
CROP_LENGTH = 768
N_COL = 16


def draw_chosen_sequence_ids(key, part):
    key = jax.random.fold_in(key, 7)
    return jax.random.permutation(key, ALIGNED_SEQS_ALL)[:CHOSEN_SEQUENCES].astype(jnp.int32)


def block_levels(rng, dims, shards, smallest, high):
    def one(axis_at, shards_of):
        steps = jax.random.uniform(jax.random.fold_in(jax.random.fold_in(rng, 6), axis_at), (shards_of,), jnp.float32, smallest / len(shards), high / len(shards))
        return jnp.repeat(jnp.exp(steps), dims[axis_at] // shards_of).reshape((-1,) + (1,) * (len(dims) - axis_at - 1))

    gain = one(*shards[0])
    for cut in shards[1:]:
        gain = gain * one(*cut)
    return gain


def noise(stream_key, extent, scale, most, cuts=(), held_as=jnp.bfloat16):
    drawn = scale * jax.random.normal(stream_key, extent, jnp.float32)
    if cuts:
        drawn = drawn * block_levels(stream_key, extent, cuts, -0.22, 0.18)
    return jnp.clip(drawn, -most, most).astype(held_as)


def setup_inputs(seed: int = 0) -> dict:
    arg_keys = jax.random.split(jax.random.key(seed), 11)
    alignment_embedding = noise(arg_keys[0], (ALIGNED_SEQS_ALL, CROP_LENGTH, CHANNEL_SPAN), 1.0, 6.0, ((1, 128),))
    chosen_sequence_ids = draw_chosen_sequence_ids(jax.random.fold_in(arg_keys[10], 71), 0)
    standardizer_scale = jnp.clip(1.0 + 0.18 * jax.random.normal(arg_keys[2], (CHANNEL_SPAN,), jnp.float32), 0.1, 1.9)
    standardizer_offset = noise(arg_keys[3], (CHANNEL_SPAN,), 0.5, 3.0, (), jnp.float32)
    first_factor_matrix = noise(arg_keys[4], (CHANNEL_SPAN, OUTER_FACTOR_DIM), CHANNEL_SPAN ** -0.5, 0.375)
    first_factor_shift = noise(arg_keys[5], (OUTER_FACTOR_DIM,), 0.5, 3.0, (), jnp.float32)
    second_factor_matrix = noise(arg_keys[6], (CHANNEL_SPAN, OUTER_FACTOR_DIM), CHANNEL_SPAN ** -0.5, 0.375)
    second_factor_shift = noise(arg_keys[7], (OUTER_FACTOR_DIM,), 0.5, 3.0, (), jnp.float32)
    final_matrix = noise(arg_keys[8], (OUTER_FACTOR_DIM * OUTER_FACTOR_DIM, TWOSITE_CHANNELS), (OUTER_FACTOR_DIM * OUTER_FACTOR_DIM) ** -0.5, 0.1875)
    twosite_delta_cotangent = noise(arg_keys[9], (CROP_LENGTH, CROP_LENGTH, TWOSITE_CHANNELS), 1.0, 6.0, ((0, 8), (1, 16)))
    return {"alignment_embedding": alignment_embedding, "chosen_sequence_ids": chosen_sequence_ids, "standardizer_scale": standardizer_scale, "standardizer_offset": standardizer_offset, "first_factor_matrix": first_factor_matrix, "first_factor_shift": first_factor_shift, "second_factor_matrix": second_factor_matrix, "second_factor_shift": second_factor_shift, "final_matrix": final_matrix, "twosite_delta_cotangent": twosite_delta_cotangent}


def rounded_values(element_numbers):
    return lax.optimization_barrier(element_numbers.astype(jnp.bfloat16)).astype(jnp.float32)

def mix(form, left, right):
    return jnp.einsum(form, left, right, precision=lax.Precision.HIGHEST)

def reference(alignment_embedding, chosen_sequence_ids, standardizer_scale, standardizer_offset, first_factor_matrix, first_factor_shift, second_factor_matrix, second_factor_shift, final_matrix, twosite_delta_cotangent):
    chosen_alignment_lines = jnp.take(alignment_embedding, chosen_sequence_ids.astype(jnp.int32), axis=0)
    element_numbers = chosen_alignment_lines.astype(jnp.float32)
    centered_input = lax.optimization_barrier(jnp.mean(element_numbers, axis=-1, keepdims=True))
    spread = lax.optimization_barrier(jnp.mean((element_numbers - centered_input) ** 2, axis=-1, keepdims=True))
    reciprocal_spread = lax.rsqrt(spread + 1e-05)
    whitened_embedding = (element_numbers - centered_input) * reciprocal_spread
    normalized_rows = rounded_values(whitened_embedding * standardizer_scale + standardizer_offset)
    proj_a = rounded_values(mix('src,cp->srp', normalized_rows, first_factor_matrix.astype(jnp.float32)) + first_factor_shift)
    proj_b = rounded_values(mix('src,cp->srp', normalized_rows, second_factor_matrix.astype(jnp.float32)) + second_factor_shift)
    total_res = proj_a.shape[1]
    i_block = RES_DEV * N_COL
    n_blocks = total_res // i_block
    blocks_a = proj_a.reshape(CHOSEN_SEQUENCES, n_blocks, i_block, OUTER_FACTOR_DIM).transpose(1, 0, 2, 3)
    grad_blocks = twosite_delta_cotangent.reshape(n_blocks, i_block, total_res, TWOSITE_CHANNELS).astype(jnp.float32)
    w_wide = final_matrix.astype(jnp.float32)

    def step(carry, pieces):
        final_matrix_slope, grad_b = carry
        a_blk, dz_blk = pieces
        outer = rounded_values(mix('sic,sje->icje', a_blk, proj_b) / CHOSEN_SEQUENCES)
        final_matrix_slope = final_matrix_slope + mix('icje,ijk->cek', outer, dz_blk)
        d_outer = rounded_values(mix('ijk,fk->ijf', dz_blk, w_wide)).reshape(i_block, total_res, OUTER_FACTOR_DIM, OUTER_FACTOR_DIM)
        grad_a = mix('ijce,sje->sic', d_outer, proj_b) / CHOSEN_SEQUENCES
        grad_b = grad_b + mix('ijce,sic->sje', d_outer, a_blk) / CHOSEN_SEQUENCES
        return ((final_matrix_slope, grad_b), grad_a)
    start = (jnp.zeros((OUTER_FACTOR_DIM, OUTER_FACTOR_DIM, TWOSITE_CHANNELS), jnp.float32), jnp.zeros((CHOSEN_SEQUENCES, total_res, OUTER_FACTOR_DIM), jnp.float32))
    (final_matrix_slope, grad_b), grad_a = lax.scan(step, start, (blocks_a, grad_blocks))
    d_a = rounded_values(grad_a.transpose(1, 0, 2, 3).reshape(CHOSEN_SEQUENCES, total_res, OUTER_FACTOR_DIM))
    d_b = rounded_values(grad_b)
    first_factor_matrix_slope = mix('src,srp->cp', normalized_rows, d_a)
    second_factor_matrix_slope = mix('src,srp->cp', normalized_rows, d_b)
    d_normed = mix('srp,cp->src', d_a, first_factor_matrix.astype(jnp.float32)) + mix('srp,cp->src', d_b, second_factor_matrix.astype(jnp.float32))
    scaled_by_coefficient = d_normed * standardizer_scale
    chosen_sequence_slope = reciprocal_spread * (scaled_by_coefficient - lax.optimization_barrier(jnp.mean(scaled_by_coefficient, axis=-1, keepdims=True)) - whitened_embedding * lax.optimization_barrier(jnp.mean(scaled_by_coefficient * whitened_embedding, axis=-1, keepdims=True)))
    return (chosen_sequence_slope.astype(jnp.bfloat16), first_factor_matrix_slope, second_factor_matrix_slope, final_matrix_slope.reshape(OUTER_FACTOR_DIM * OUTER_FACTOR_DIM, TWOSITE_CHANNELS))
```

```python
import functools

import jax
import jax.numpy as jnp
from jax import lax
from jax.experimental import pallas as pl
from jax.experimental.pallas import tpu as pltpu
from jax.sharding import PartitionSpec as P

CHOSEN_SEQUENCES = 128
SLOT = 8

BF = jnp.bfloat16
F32 = jnp.float32
NN = (((1,), (0,)), ((), ()))
NT = (((1,), (1,)), ((), ()))


def dot(left, right, dims=NN):
    return lax.dot_general(left, right, dims, preferred_element_type=F32)


def kernel(
    emb_ref, ids_ref, scale_ref, offset_ref, w_a_ref, w_b_ref, shift_ref, final_ref, dz_ref,
    slope_ref, grad_a_ref, grad_b_ref, grad_w_ref,
    xhat_ref, inv_ref, normed_ref, dzf_ref, dzb_ref, d_ref, o_ref,
    abuf, bsend, bbuf, atf_ref, at_ref, bt_ref, daf_ref, sa, ra, sb, rb,
    sw, rw, sw2, rw2, fw, wacc_ref, sp, rp, sp2, rp2, fp,
    ssem_a, rsem_a, ssem_b, rsem_b, ssem_ra, rsem_ra, ssem_rb, rsem_rb,
    ssem_w, rsem_w, ssem_w2, rsem_w2, ssem_w3, rsem_w3,
    ssem_p, rsem_p, ssem_p2, rsem_p2, ssem_p3, rsem_p3,
):
    n_row, n_col = bbuf.shape[0], abuf.shape[0]
    n_res, n_sel, width = normed_ref.shape
    rank = w_a_ref.shape[0]
    n_j = n_row * n_res
    lanes = n_col * SLOT
    chunk = n_res * rank
    row, col = lax.axis_index("row"), lax.axis_index("col")
    me = row * n_col + col
    b_col, b_slot = me // n_row, me % n_row

    def copy(src, dst, send_sem, recv_sem, device):
        return pltpu.make_async_remote_copy(
            src_ref=src, dst_ref=dst, send_sem=send_sem, recv_sem=recv_sem,
            device_id=device, device_id_type=pl.DeviceIdType.MESH,
        )

    def each(count, body):
        lax.fori_loop(0, count, lambda i, _: (body(i), None)[1], None)

    def col_peer(t):
        return lax.rem(col + t, n_col)

    def row_peer(t):
        return lax.rem(row + t, n_row)

    def source(k):
        block = n_row * col + k
        return block // n_col, block % n_col

    barrier = pltpu.get_barrier_semaphore()

    def greet(device):
        pl.semaphore_signal(barrier, inc=1, device_id=device, device_id_type=pl.DeviceIdType.MESH)

    each(n_col - 1, lambda t: greet((row, col_peer(t + 1))))
    each(n_row - 1, lambda t: greet((row_peer(t + 1), col)))

    def greet_b(k):
        src = source(k)

        @pl.when(n_row * col + k != me)
        def _():
            greet(src)

        @pl.when(jnp.logical_or(k != row, b_col != col))
        def _():
            greet((k, b_col))

    each(n_row, greet_b)

    picks = (
        lax.broadcasted_iota(jnp.int32, (n_sel, emb_ref.shape[1]), 1) == ids_ref[...]
    ).astype(F32).astype(BF)
    w_both = jnp.concatenate([w_a_ref[...], w_b_ref[...]], axis=0)
    for r in range(n_res):
        x = dot(picks, emb_ref[r])
        centred = x - jnp.mean(x, axis=-1, keepdims=True)
        inverse = lax.rsqrt(jnp.mean(centred * centred, axis=-1, keepdims=True) + 1e-05)
        xhat = centred * inverse
        xhat_ref[r] = xhat
        inv_ref[r] = inverse
        normed = (xhat * scale_ref[...] + offset_ref[...]).astype(BF)
        normed_ref[r] = normed
        proj = (dot(w_both, normed, NT) + shift_ref[...]).astype(BF)
        abuf[col, r * rank : (r + 1) * rank, :] = proj[:rank]
        bsend[r * rank : (r + 1) * rank, :] = proj[rank:]

    self_b = jnp.where(b_col == col, 1, 0)
    pl.semaphore_wait(barrier, (n_col - 1) + (n_row - 1) + 2 * (n_row - self_b))

    def b_copy(k):
        return copy(bsend, bbuf.at[b_slot], ssem_b.at[k], rsem_b.at[b_slot], (k, b_col))

    def send_b(t):
        k = row_peer(t)

        @pl.when(jnp.logical_or(k != row, b_col != col))
        def _():
            b_copy(k).start()

    @pl.when(b_col == col)
    def _():
        bbuf[b_slot] = bsend[...]

    each(n_row, send_b)

    def a_copy(t, peer):
        return copy(abuf.at[col], abuf.at[col], ssem_a.at[t], rsem_a.at[col], (row, peer))

    each(n_col - 1, lambda t: a_copy(t, col_peer(t + 1)).start())

    n_i, j_width, k_width = dz_ref.shape
    dzf_ref[pl.ds(0, n_i * j_width), :] = dz_ref[...].astype(F32).reshape(n_i * j_width, k_width)
    dzf_ref[pl.ds(n_i * j_width, 2 * j_width), :] = jnp.zeros((2 * j_width, k_width), F32)
    atf_ref[...] = jnp.zeros(atf_ref.shape, F32)

    def spread(j):
        rows = [
            dzf_ref[pl.ds(n_res * q * j_width + j, SLOT, stride=j_width), :] for q in range(n_col)
        ]
        dzb_ref[j] = jnp.concatenate(rows, axis=0).astype(BF)

    each(n_j, spread)

    def d_step(step):
        pair = dzb_ref[pl.ds(2 * step, 2)].reshape(2 * lanes, k_width)
        d = dot(final_ref[...], pair, NT).astype(BF)
        for q in range(2):
            at = pl.ds(pl.multiple_of((2 * step + q) * rank, rank), rank)
            d_ref[:, at, :] = d[:, q * lanes : (q + 1) * lanes].reshape(rank, rank, lanes)

    each(n_j // 2, d_step)

    def wait_b(k):
        @pl.when(n_row * col + k != me)
        def _():
            copy(bsend, bbuf.at[k], ssem_b.at[k], rsem_b.at[k], source(k)).wait_recv()

    each(n_row, wait_b)
    right_t = bbuf[...].reshape(n_j * rank, n_sel)
    bt_ref[...] = right_t.T

    def part_a_step(step):
        d = jnp.concatenate([d_ref[2 * step], d_ref[2 * step + 1]], axis=1)
        part = dot(bt_ref[...], d) * (1.0 / CHOSEN_SEQUENCES)
        for q in range(2):
            at = pl.ds(pl.multiple_of((2 * step + q) * lanes, lanes), lanes)
            daf_ref[at, :] = part[:, q * lanes : (q + 1) * lanes].T

    each(rank // 2, part_a_step)

    def ra_copy(t, peer):
        return copy(sa.at[peer], ra.at[col], ssem_ra.at[t], rsem_ra.at[col], (row, peer))

    def a_chunk(q):
        return [
            daf_ref[pl.ds(q * SLOT + r, rank, stride=lanes), :].astype(BF) for r in range(n_res)
        ]

    def send_part_a(t):
        peer = col_peer(t + 1)
        for r, piece in enumerate(a_chunk(peer)):
            sa[peer, r * rank : (r + 1) * rank, :] = piece
        ra_copy(t, peer).start()

    each(n_col - 1, send_part_a)
    for r, piece in enumerate(a_chunk(col)):
        ra[col, r * rank : (r + 1) * rank, :] = piece

    def take_a(q):
        for r in range(n_res):
            atf_ref[pl.ds(q * SLOT + r, rank, stride=lanes), :] = abuf[
                q, r * rank : (r + 1) * rank, :
            ].astype(F32)

    take_a(col)

    def wait_a(t):
        q = col_peer(n_col - 1 - t)
        copy(abuf.at[q], abuf.at[q], ssem_a.at[t], rsem_a.at[q], (row, q)).wait_recv()
        take_a(q)

    each(n_col - 1, wait_a)

    def cast_a(c):
        at = pl.ds(pl.multiple_of(c * 4 * lanes, 4 * lanes), 4 * lanes)
        at_ref[at, :] = atf_ref[at, :].astype(BF)

    each(rank // 4, cast_a)

    def rb_copy(k, device):
        return copy(sb.at[k], rb.at[row], ssem_rb.at[k], rsem_rb.at[row], device)

    def part_b_step(k):
        at = pl.ds(pl.multiple_of(k * chunk, chunk), chunk)
        total = jnp.zeros((chunk, n_sel), F32)
        for c in range(0, rank, 2):
            d = jnp.concatenate([d_ref[c, at, :], d_ref[c + 1, at, :]], axis=1)
            total += dot(d, at_ref[c * lanes : (c + 2) * lanes, :])
        total = (total * (1.0 / CHOSEN_SEQUENCES)).astype(BF)
        sb[k] = total

        @pl.when(n_row * col + k == me)
        def _():
            rb[row] = total

        @pl.when(n_row * col + k != me)
        def _():
            rb_copy(k, source(k)).start()

    each(n_row, part_b_step)

    def o_step(step):
        at = pl.ds(pl.multiple_of(2 * step * lanes, 2 * lanes), 2 * lanes)
        o = dot(bbuf[...].reshape(n_j * rank, n_sel), at_ref[at, :], NT).astype(BF)
        o_ref[2 * step] = o[:, :lanes]
        o_ref[2 * step + 1] = o[:, lanes:]

    each(rank // 2, o_step)

    wacc_ref[...] = jnp.zeros(wacc_ref.shape, F32)

    def w_step(step):
        pieces = []
        for q in range(4):
            at = pl.ds(pl.multiple_of((4 * step + q) * rank, rank), rank)
            pieces.append(o_ref[:, at, :].reshape(rank * rank, lanes))
        z = dzb_ref[pl.ds(4 * step, 4)].reshape(4 * lanes, k_width)
        wacc_ref[...] += dot(jnp.concatenate(pieces, axis=1), z)

    each(n_j // 4, w_step)
    sw[...] = (wacc_ref[...] * (1.0 / CHOSEN_SEQUENCES)).astype(BF).reshape(sw.shape)

    def w_copy(t, peer):
        return copy(sw.at[peer], rw.at[col], ssem_w.at[t], rsem_w.at[col], (row, peer))

    each(n_col - 1, lambda t: w_copy(t, col_peer(t + 1)).start())
    rw[col] = sw[col]

    def wait_ra(t):
        q = col_peer(n_col - 1 - t)
        copy(sa.at[q], ra.at[q], ssem_ra.at[t], rsem_ra.at[q], (row, q)).wait_recv()

    each(n_col - 1, wait_ra)

    def wait_rb(k):
        @pl.when(jnp.logical_or(k != row, b_col != col))
        def _():
            copy(sb.at[k], rb.at[k], ssem_rb.at[k], rsem_rb.at[k], (k, b_col)).wait_recv()

    each(n_row, wait_rb)

    d_a = jnp.sum(ra[...].astype(F32), axis=0).astype(BF)
    d_b = jnp.sum(rb[...].astype(F32), axis=0).astype(BF)
    d_both = [
        jnp.concatenate(
            [d_a[r * rank : (r + 1) * rank], d_b[r * rank : (r + 1) * rank]], axis=0
        )
        for r in range(n_res)
    ]
    part_p = jnp.zeros((2 * rank, width), F32)
    for r in range(n_res):
        part_p += dot(d_both[r], normed_ref[r])
    half = width // 2
    sp[...] = jnp.concatenate([part_p[:, :half], part_p[:, half:]], axis=0).reshape(sp.shape)

    def p_copy(t, peer):
        return copy(sp.at[peer], rp.at[col], ssem_p.at[t], rsem_p.at[col], (row, peer))

    each(n_col - 1, lambda t: p_copy(t, col_peer(t + 1)).start())
    rp[col] = sp[col]

    def wait_w(t):
        q = col_peer(n_col - 1 - t)
        copy(sw.at[q], rw.at[q], ssem_w.at[t], rsem_w.at[q], (row, q)).wait_recv()

    each(n_col - 1, wait_w)
    sw2[...] = jnp.sum(rw[...].astype(F32), axis=0).astype(BF)
    rw2[row] = sw2[...]

    def w2_copy(t, peer):
        return copy(sw2, rw2.at[row], ssem_w2.at[t], rsem_w2.at[row], (peer, col))

    each(n_row - 1, lambda t: w2_copy(t, row_peer(t + 1)).start())

    def layer_norm_back(r):
        g = lax.dot_general(
            d_both[r], w_both, (((0,), (0,)), ((), ())), preferred_element_type=F32
        )
        g = g * scale_ref[...]
        xhat = xhat_ref[r]
        slope = inv_ref[r] * (
            g
            - jnp.mean(g, axis=-1, keepdims=True)
            - xhat * jnp.mean(g * xhat, axis=-1, keepdims=True)
        )
        slope_ref[r] = slope.astype(BF)

    for r in range(n_res // 2):
        layer_norm_back(r)

    def wait_p(t):
        q = col_peer(n_col - 1 - t)
        copy(sp.at[q], rp.at[q], ssem_p.at[t], rsem_p.at[q], (row, q)).wait_recv()

    each(n_col - 1, wait_p)
    sp2[...] = jnp.sum(rp[...], axis=0)
    rp2[row] = sp2[...]

    def p2_copy(t, peer):
        return copy(sp2, rp2.at[row], ssem_p2.at[t], rsem_p2.at[row], (peer, col))

    each(n_row - 1, lambda t: p2_copy(t, row_peer(t + 1)).start())

    def wait_w2(t):
        q = row_peer(n_row - 1 - t)
        copy(sw2, rw2.at[q], ssem_w2.at[t], rsem_w2.at[q], (q, col)).wait_recv()

    each(n_row - 1, wait_w2)
    fw[col] = jnp.sum(rw2[...].astype(F32), axis=0).astype(BF)

    def w3_copy(t, peer):
        return copy(fw.at[col], fw.at[col], ssem_w3.at[t], rsem_w3.at[col], (row, peer))

    each(n_col - 1, lambda t: w3_copy(t, col_peer(t + 1)).start())

    for r in range(n_res // 2, n_res):
        layer_norm_back(r)

    def wait_p2(t):
        q = row_peer(n_row - 1 - t)
        copy(sp2, rp2.at[q], ssem_p2.at[t], rsem_p2.at[q], (q, col)).wait_recv()

    each(n_row - 1, wait_p2)
    fp[col] = jnp.sum(rp2[...], axis=0)

    def p3_copy(t, peer):
        return copy(fp.at[col], fp.at[col], ssem_p3.at[t], rsem_p3.at[col], (row, peer))

    each(n_col - 1, lambda t: p3_copy(t, col_peer(t + 1)).start())

    def wait_w3(t):
        q = col_peer(n_col - 1 - t)
        copy(fw.at[q], fw.at[q], ssem_w3.at[t], rsem_w3.at[q], (row, q)).wait_recv()

    each(n_col - 1, wait_w3)
    grad_w_ref[...] = fw[...].astype(F32).reshape(grad_w_ref.shape)

    def wait_p3(t):
        q = col_peer(n_col - 1 - t)
        copy(fp.at[q], fp.at[q], ssem_p3.at[t], rsem_p3.at[q], (row, q)).wait_recv()

    each(n_col - 1, wait_p3)
    both = fp[...].reshape(4 * rank, half)
    grad_a_ref[...] = jnp.concatenate([both[:rank], both[2 * rank : 3 * rank]], axis=1)
    grad_b_ref[...] = jnp.concatenate([both[rank : 2 * rank], both[3 * rank :]], axis=1)

    def sent_b(k):
        @pl.when(jnp.logical_or(k != row, b_col != col))
        def _():
            b_copy(k).wait_send()

        @pl.when(n_row * col + k != me)
        def _():
            rb_copy(k, source(k)).wait_send()

    each(n_row, sent_b)

    def sent_col(t):
        peer = col_peer(t + 1)
        for made in (a_copy, ra_copy, w_copy, w3_copy, p_copy, p3_copy):
            made(t, peer).wait_send()

    each(n_col - 1, sent_col)

    def sent_row(t):
        peer = row_peer(t + 1)
        for made in (w2_copy, p2_copy):
            made(t, peer).wait_send()

    each(n_row - 1, sent_row)


def shards(
    n_row,
    n_col,
    alignment_embedding,
    chosen_sequence_ids,
    standardizer_scale,
    standardizer_offset,
    first_factor_matrix,
    first_factor_shift,
    second_factor_matrix,
    second_factor_shift,
    final_matrix,
    twosite_delta_cotangent,
):
    width, rank = first_factor_matrix.shape
    n_sel = chosen_sequence_ids.shape[0]
    n_res = alignment_embedding.shape[1]
    n_i, n_j, k_width = twosite_delta_cotangent.shape
    lanes = n_col * SLOT
    chunk = n_res * rank
    w_rows = rank * rank // n_col
    p_rows = 4 * rank // n_col
    dma = lambda n: pltpu.SemaphoreType.DMA((n,))
    vmem = pltpu.VMEM
    scratch = [
        vmem((n_res, n_sel, width), F32),
        vmem((n_res, n_sel, 1), F32),
        vmem((n_res, n_sel, width), BF),
        vmem(((n_i + 2) * n_j, k_width), F32),
        vmem((n_j, lanes, k_width), BF),
        vmem((rank, n_j * rank, lanes), BF),
        vmem((rank, n_j * rank, lanes), BF),
        vmem((n_col, chunk, n_sel), BF),
        vmem((chunk, n_sel), BF),
        vmem((n_row, chunk, n_sel), BF),
        vmem((rank * lanes, n_sel), F32),
        vmem((rank * lanes, n_sel), BF),
        vmem((n_sel, n_j * rank), BF),
        vmem((rank * lanes, n_sel), F32),
        vmem((n_col, chunk, n_sel), BF),
        vmem((n_col, chunk, n_sel), BF),
        vmem((n_row, chunk, n_sel), BF),
        vmem((n_row, chunk, n_sel), BF),
        vmem((n_col, w_rows, k_width), BF),
        vmem((n_col, w_rows, k_width), BF),
        vmem((w_rows, k_width), BF),
        vmem((n_row, w_rows, k_width), BF),
        vmem((n_col, w_rows, k_width), BF),
        vmem((rank * rank, k_width), F32),
        vmem((n_col, p_rows, width // 2), F32),
        vmem((n_col, p_rows, width // 2), F32),
        vmem((p_rows, width // 2), F32),
        vmem((n_row, p_rows, width // 2), F32),
        vmem((n_col, p_rows, width // 2), F32),
        *[dma(n) for n in (n_col, n_col, n_row, n_row, n_col, n_col, n_row, n_row)],
        *[dma(n) for n in (n_col, n_col, n_row, n_row, n_col, n_col)],
        *[dma(n) for n in (n_col, n_col, n_row, n_row, n_col, n_col)],
    ]
    whole = pl.BlockSpec(memory_space=pltpu.VMEM)
    shift = jnp.concatenate([first_factor_shift, second_factor_shift]).reshape(2 * rank, 1)
    slope, grad_a, grad_b, grad_w = pl.pallas_call(
        kernel,
        out_shape=(
            jax.ShapeDtypeStruct((n_res, n_sel, width), BF),
            jax.ShapeDtypeStruct((rank, width), F32),
            jax.ShapeDtypeStruct((rank, width), F32),
            jax.ShapeDtypeStruct((rank * rank, k_width), F32),
        ),
        in_specs=[whole] * 9,
        out_specs=(whole,) * 4,
        scratch_shapes=scratch,
        compiler_params=pltpu.CompilerParams(
            collective_id=0, has_side_effects=True, vmem_limit_bytes=60 * 1024 * 1024
        ),
    )(
        alignment_embedding.transpose(1, 0, 2),
        chosen_sequence_ids.reshape(n_sel, 1),
        standardizer_scale.reshape(1, width),
        standardizer_offset.reshape(1, width),
        first_factor_matrix.T,
        second_factor_matrix.T,
        shift,
        final_matrix,
        twosite_delta_cotangent,
    )
    return slope.transpose(1, 0, 2), grad_a.T, grad_b.T, grad_w


def solution(mesh):
    return jax.shard_map(
        functools.partial(shards, mesh.shape["row"], mesh.shape["col"]),
        mesh=mesh,
        in_specs=(
            P(None, ("row", "col"), None),
            P(),
            P(),
            P(),
            P(),
            P(),
            P(),
            P(),
            P(),
            P("row", "col", None),
        ),
        out_specs=(P(None, ("row", "col"), None), P(), P(), P()),
        check_vma=False,
    )
```

```python
import functools

import jax
import jax.numpy as jnp
from jax import lax
from jax.experimental import pallas as pl
from jax.experimental.pallas import tpu as pltpu
from jax.sharding import PartitionSpec as P

CHOSEN_SEQUENCES = 128
SLOT = 8

BF = jnp.bfloat16
F32 = jnp.float32
NN = (((1,), (0,)), ((), ()))
NT = (((1,), (1,)), ((), ()))


def dot(left, right, dims=NN):
    return lax.dot_general(left, right, dims, preferred_element_type=F32)


def kernel(
    emb_ref, ids_ref, scale_ref, offset_ref, w_a_ref, w_b_ref, shift_ref, final_ref, dz_ref,
    slope_ref, sums_ref,
    xhat_ref, inv_ref, normed_ref, dzf_ref, dzb_ref, d_ref, o_ref,
    abuf, bsend, bbuf, atf_ref, at_ref, bt_ref, daf_ref, sa, ra0, sa1, ra1, sb, rb, wacc_ref,
    st0, rt0, st1, rt1, st2, rt2,
    ssem_a, rsem_a, ssem_a2, rsem_a2, ssem_b, rsem_b, ssem_ra, rsem_ra, ssem_rb, rsem_rb,
    ssem_t1, rsem_t1, ssem_t2, rsem_t2, ssem_t3, rsem_t3, sib_sems,
):
    n_row, n_col = bbuf.shape[0], abuf.shape[0]
    n_chip = n_col // 2
    n_res, n_sel, width = normed_ref.shape
    rank = w_a_ref.shape[0]
    n_j = n_row * n_res
    lanes = n_col * SLOT
    chunk = n_res * rank
    row, col = lax.axis_index("row"), lax.axis_index("col")
    me = row * n_col + col
    b_col, b_slot = me // n_row, me % n_row
    chip, core = col // 2, col % 2
    other = 1 - core
    sibling = (row, col + 1 - 2 * core)

    def copy(src, dst, send_sem, recv_sem, device):
        return pltpu.make_async_remote_copy(
            src_ref=src, dst_ref=dst, send_sem=send_sem, recv_sem=recv_sem,
            device_id=device, device_id_type=pl.DeviceIdType.MESH,
        )

    def each(count, body):
        lax.fori_loop(0, count, lambda i, _: (body(i), None)[1], None)

    def chip_peer(t):
        return lax.rem(chip + t, n_chip)

    def at_chip(q):
        return (row, 2 * q + core)

    def row_peer(t):
        return lax.rem(row + t, n_row)

    def source(k):
        block = n_row * col + k
        return block // n_col, block % n_col

    barrier = pltpu.get_barrier_semaphore()

    def greet(device):
        pl.semaphore_signal(barrier, inc=1, device_id=device, device_id_type=pl.DeviceIdType.MESH)

    greet(sibling)
    each(n_chip - 1, lambda t: greet(at_chip(chip_peer(t + 1))))
    each(n_row - 1, lambda t: greet((row_peer(t + 1), col)))

    def greet_b(k):
        src = source(k)

        @pl.when(n_row * col + k != me)
        def _():
            greet(src)

        @pl.when(jnp.logical_or(k != row, b_col != col))
        def _():
            greet((k, b_col))

    each(n_row, greet_b)

    n_all = emb_ref.shape[1]
    ids = jnp.broadcast_to(ids_ref[...], (n_sel, n_sel)).T
    ids = jnp.concatenate([ids] * (n_all // n_sel), axis=1)
    picks = (lax.broadcasted_iota(jnp.int32, (n_sel, n_all), 1) == ids).astype(F32).astype(BF)
    w_both = jnp.concatenate([w_a_ref[...], w_b_ref[...]], axis=0)
    for r in range(n_res):
        x = dot(picks, emb_ref[r])
        centred = x - jnp.mean(x, axis=-1, keepdims=True)
        inverse = lax.rsqrt(jnp.mean(centred * centred, axis=-1, keepdims=True) + 1e-05)
        xhat = centred * inverse
        xhat_ref[r] = xhat
        inv_ref[r] = inverse
        normed = (xhat * scale_ref[...] + offset_ref[...]).astype(BF)
        normed_ref[r] = normed
        proj = (dot(w_both, normed, NT) + shift_ref[...]).astype(BF)
        abuf[col, r * rank : (r + 1) * rank, :] = proj[:rank]
        bsend[r * rank : (r + 1) * rank, :] = proj[rank:]

    self_b = jnp.where(b_col == col, 1, 0)
    pl.semaphore_wait(barrier, n_chip + (n_row - 1) + 2 * (n_row - self_b))

    def b_copy(k):
        return copy(bsend, bbuf.at[b_slot], ssem_b.at[k], rsem_b.at[b_slot], (k, b_col))

    def send_b(t):
        k = row_peer(t)

        @pl.when(jnp.logical_or(k != row, b_col != col))
        def _():
            b_copy(k).start()

    @pl.when(b_col == col)
    def _():
        bbuf[b_slot] = bsend[...]

    each(n_row, send_b)

    def a_copy(t, q):
        return copy(abuf.at[col], abuf.at[col], ssem_a.at[t], rsem_a.at[chip], at_chip(q))

    def a_forward(q):
        block = abuf.at[2 * q + core]
        return copy(block, block, ssem_a2.at[q], rsem_a2.at[q], sibling)

    each(n_chip - 1, lambda t: a_copy(t, chip_peer(t + 1)).start())
    a_forward(chip).start()

    n_i, j_width, k_width = dz_ref.shape
    dzf_ref[pl.ds(0, n_i * j_width), :] = dz_ref[...].astype(F32).reshape(n_i * j_width, k_width)
    dzf_ref[pl.ds(n_i * j_width, 2 * j_width), :] = jnp.zeros((2 * j_width, k_width), F32)
    atf_ref[...] = jnp.zeros(atf_ref.shape, F32)

    def spread(j):
        rows = [
            dzf_ref[pl.ds(n_res * q * j_width + j, SLOT, stride=j_width), :] for q in range(n_col)
        ]
        dzb_ref[j] = jnp.concatenate(rows, axis=0).astype(BF)

    each(n_j, spread)

    def d_step(step):
        pair = dzb_ref[pl.ds(2 * step, 2)].reshape(2 * lanes, k_width)
        d = dot(final_ref[...], pair, NT).astype(BF)
        for q in range(2):
            at = pl.ds(pl.multiple_of((2 * step + q) * rank, rank), rank)
            d_ref[:, at, :] = d[:, q * lanes : (q + 1) * lanes].reshape(rank, rank, lanes)

    each(n_j // 2, d_step)

    def pass_a(t):
        q = chip_peer(n_chip - 1 - t)
        block = abuf.at[2 * q + core]
        copy(block, block, ssem_a.at[t], rsem_a.at[q], at_chip(q)).wait_recv()
        a_forward(q).start()

    each(n_chip - 1, pass_a)

    def wait_b(k):
        @pl.when(n_row * col + k != me)
        def _():
            copy(bsend, bbuf.at[k], ssem_b.at[k], rsem_b.at[k], source(k)).wait_recv()

    each(n_row, wait_b)
    right_t = bbuf[...].reshape(n_j * rank, n_sel)
    bt_ref[...] = right_t.T

    def part_a_step(step):
        d = jnp.concatenate([d_ref[2 * step], d_ref[2 * step + 1]], axis=1)
        part = dot(bt_ref[...], d) * (1.0 / CHOSEN_SEQUENCES)
        for q in range(2):
            at = pl.ds(pl.multiple_of((2 * step + q) * lanes, lanes), lanes)
            daf_ref[at, :] = part[:, q * lanes : (q + 1) * lanes].T

    each(rank // 2, part_a_step)

    def pack_a(q):
        for k in range(2):
            for r in range(n_res):
                sa[k, q, r * rank : (r + 1) * rank, :] = daf_ref[
                    pl.ds((2 * q + k) * SLOT + r, rank, stride=lanes), :
                ].astype(BF)

    each(n_chip, pack_a)

    def sib_copy(i, src, dst):
        return copy(src, dst, sib_sems.at[i], sib_sems.at[i + 1], sibling)

    ra_sib = sib_copy(0, sa.at[other], ra0)
    ra_sib.start()

    def take_a(q):
        for r in range(n_res):
            atf_ref[pl.ds(q * SLOT + r, rank, stride=lanes), :] = abuf[
                q, r * rank : (r + 1) * rank, :
            ].astype(F32)

    def wait_a(q):
        block = abuf.at[2 * q + other]
        copy(block, block, ssem_a2.at[q], rsem_a2.at[q], sibling).wait_recv()
        take_a(2 * q)
        take_a(2 * q + 1)

    each(n_chip, wait_a)

    def cast_a(c):
        at = pl.ds(pl.multiple_of(c * 4 * lanes, 4 * lanes), 4 * lanes)
        at_ref[at, :] = atf_ref[at, :].astype(BF)

    each(rank // 4, cast_a)

    def ra_copy(t, q):
        return copy(sa1.at[q], ra1.at[chip], ssem_ra.at[t], rsem_ra.at[chip], at_chip(q))

    ra_sib.wait_recv()

    def send_part_a(t):
        q = chip_peer(t + 1)
        sa1[q] = (sa[core, q].astype(F32) + ra0[q].astype(F32)).astype(BF)
        ra_copy(t, q).start()

    each(n_chip - 1, send_part_a)
    ra1[chip] = (sa[core, chip].astype(F32) + ra0[chip].astype(F32)).astype(BF)

    def rb_copy(k, device):
        return copy(sb.at[k], rb.at[row], ssem_rb.at[k], rsem_rb.at[row], device)

    def part_b_step(k):
        at = pl.ds(pl.multiple_of(k * chunk, chunk), chunk)
        total = jnp.zeros((chunk, n_sel), F32)
        for c in range(0, rank, 2):
            d = jnp.concatenate([d_ref[c, at, :], d_ref[c + 1, at, :]], axis=1)
            total += dot(d, at_ref[c * lanes : (c + 2) * lanes, :])
        total = (total * (1.0 / CHOSEN_SEQUENCES)).astype(BF)
        sb[k] = total

        @pl.when(n_row * col + k == me)
        def _():
            rb[row] = total

        @pl.when(n_row * col + k != me)
        def _():
            rb_copy(k, source(k)).start()

    each(n_row, part_b_step)

    def o_step(step):
        at = pl.ds(pl.multiple_of(2 * step * lanes, 2 * lanes), 2 * lanes)
        o = dot(bbuf[...].reshape(n_j * rank, n_sel), at_ref[at, :], NT).astype(BF)
        o_ref[2 * step] = o[:, :lanes]
        o_ref[2 * step + 1] = o[:, lanes:]

    each(rank // 2, o_step)

    wacc_ref[...] = jnp.zeros(wacc_ref.shape, F32)

    def w_step(step):
        pieces = []
        for q in range(4):
            at = pl.ds(pl.multiple_of((4 * step + q) * rank, rank), rank)
            pieces.append(o_ref[:, at, :].reshape(rank * rank, lanes))
        z = dzb_ref[pl.ds(4 * step, 4)].reshape(4 * lanes, k_width)
        wacc_ref[...] += dot(jnp.concatenate(pieces, axis=1), z).reshape(wacc_ref.shape)

    each(n_j // 4, w_step)

    def wait_ra(t):
        q = chip_peer(n_chip - 1 - t)
        copy(sa1.at[q], ra1.at[q], ssem_ra.at[t], rsem_ra.at[q], at_chip(q)).wait_recv()

    each(n_chip - 1, wait_ra)

    def wait_rb(k):
        @pl.when(jnp.logical_or(k != row, b_col != col))
        def _():
            copy(sb.at[k], rb.at[k], ssem_rb.at[k], rsem_rb.at[k], (k, b_col)).wait_recv()

    each(n_row, wait_rb)

    d_a = jnp.sum(ra1[...].astype(F32), axis=0).astype(BF)
    d_b = jnp.sum(rb[...].astype(F32), axis=0).astype(BF)
    d_both = [
        jnp.concatenate(
            [d_a[r * rank : (r + 1) * rank], d_b[r * rank : (r + 1) * rank]], axis=0
        )
        for r in range(n_res)
    ]
    part_p = jnp.zeros((2 * rank, width), F32)
    for r in range(n_res):
        part_p += dot(d_both[r], normed_ref[r])
    half = width // 2
    part_p = jnp.concatenate([part_p[:, :half], part_p[:, half:]], axis=0)

    w_rows, p_rows = rank * rank // n_col, 4 * rank // n_col

    def fill(i):
        st0[i, :w_rows, :] = (wacc_ref[i] * (1.0 / CHOSEN_SEQUENCES)).astype(BF)

    each(n_col, fill)
    for i in range(n_col):
        st0[i, w_rows : w_rows + p_rows, :] = part_p[i * p_rows : (i + 1) * p_rows].astype(BF)
        st0[i, w_rows + p_rows :, :] = jnp.zeros((st0.shape[1] - w_rows - p_rows, half), BF)
    t_sib = sib_copy(2, st0.at[pl.ds(other * n_chip, n_chip)], rt0)
    t_sib.start()

    def layer_norm_back(r):
        g = lax.dot_general(
            d_both[r], w_both, (((0,), (0,)), ((), ())), preferred_element_type=F32
        )
        g = g * scale_ref[...]
        xhat = xhat_ref[r]
        slope = inv_ref[r] * (
            g
            - jnp.mean(g, axis=-1, keepdims=True)
            - xhat * jnp.mean(g * xhat, axis=-1, keepdims=True)
        )
        slope_ref[r] = slope.astype(BF)

    layer_norm_back(0)
    t_sib.wait_recv()

    def t1_copy(t, q):
        return copy(st1.at[q], rt1.at[chip], ssem_t1.at[t], rsem_t1.at[chip], at_chip(q))

    def send_t1(t):
        q = chip_peer(t + 1)
        st1[q] = (st0[core * n_chip + q].astype(F32) + rt0[q].astype(F32)).astype(BF)
        t1_copy(t, q).start()

    each(n_chip - 1, send_t1)
    rt1[chip] = (st0[core * n_chip + chip].astype(F32) + rt0[chip].astype(F32)).astype(BF)
    layer_norm_back(1)
    layer_norm_back(2)

    def wait_t1(t):
        q = chip_peer(n_chip - 1 - t)
        copy(st1.at[q], rt1.at[q], ssem_t1.at[t], rsem_t1.at[q], at_chip(q)).wait_recv()

    each(n_chip - 1, wait_t1)
    st2[...] = jnp.sum(rt1[...].astype(F32), axis=0).astype(BF)
    rt2[row] = st2[...]

    def t2_copy(t, q):
        return copy(st2, rt2.at[row], ssem_t2.at[t], rsem_t2.at[row], (q, col))

    each(n_row - 1, lambda t: t2_copy(t, row_peer(t + 1)).start())
    layer_norm_back(3)
    layer_norm_back(4)

    def wait_t2(t):
        q = row_peer(n_row - 1 - t)
        copy(st2, rt2.at[q], ssem_t2.at[t], rsem_t2.at[q], (q, col)).wait_recv()

    each(n_row - 1, wait_t2)
    sums_ref[core * n_chip + chip] = jnp.sum(rt2[...].astype(F32), axis=0).astype(BF)

    def t3_copy(t, q):
        block = sums_ref.at[core * n_chip + chip]
        return copy(block, block, ssem_t3.at[t], rsem_t3.at[chip], at_chip(q))

    each(n_chip - 1, lambda t: t3_copy(t, chip_peer(t + 1)).start())
    layer_norm_back(5)

    def wait_t3(t):
        q = chip_peer(n_chip - 1 - t)
        block = sums_ref.at[core * n_chip + q]
        copy(block, block, ssem_t3.at[t], rsem_t3.at[q], at_chip(q)).wait_recv()

    each(n_chip - 1, wait_t3)
    mine = sums_ref.at[pl.ds(core * n_chip, n_chip)]
    theirs = sums_ref.at[pl.ds(other * n_chip, n_chip)]
    sib_copy(4, mine, mine).start()
    sib_copy(4, theirs, theirs).wait_recv()

    def sent_b(k):
        @pl.when(jnp.logical_or(k != row, b_col != col))
        def _():
            b_copy(k).wait_send()

        @pl.when(n_row * col + k != me)
        def _():
            rb_copy(k, source(k)).wait_send()

    each(n_row, sent_b)

    def sent_chip(t):
        q = chip_peer(t + 1)
        for made in (a_copy, ra_copy, t1_copy, t3_copy):
            made(t, q).wait_send()

    each(n_chip - 1, sent_chip)
    each(n_chip, lambda q: a_forward(q).wait_send())
    each(n_row - 1, lambda t: t2_copy(t, row_peer(t + 1)).wait_send())
    ra_sib.wait_send()
    t_sib.wait_send()
    sib_copy(4, mine, mine).wait_send()


def last_kernel(slope_ref, sums_ref, out_ref, grad_a_ref, grad_b_ref, grad_w_ref):
    out_ref[...] = slope_ref[...]
    rank = grad_a_ref.shape[0]
    n = sums_ref.shape[0]
    w_rows, p_rows = rank * rank // n, 4 * rank // n
    pieces = []
    for i in range(n):
        piece = sums_ref[i].astype(F32)
        grad_w_ref[i * w_rows : (i + 1) * w_rows, :] = piece[:w_rows]
        pieces.append(piece[w_rows : w_rows + p_rows])
    both = jnp.concatenate(pieces, axis=0)
    grad_a_ref[...] = jnp.concatenate([both[:rank], both[2 * rank : 3 * rank]], axis=1)
    grad_b_ref[...] = jnp.concatenate([both[rank : 2 * rank], both[3 * rank :]], axis=1)


def shards(
    n_row,
    n_col,
    alignment_embedding,
    chosen_sequence_ids,
    standardizer_scale,
    standardizer_offset,
    first_factor_matrix,
    first_factor_shift,
    second_factor_matrix,
    second_factor_shift,
    final_matrix,
    twosite_delta_cotangent,
):
    width, rank = first_factor_matrix.shape
    n_sel = chosen_sequence_ids.shape[0]
    n_res = alignment_embedding.shape[1]
    n_i, n_j, k_width = twosite_delta_cotangent.shape
    lanes = n_col * SLOT
    chunk = n_res * rank
    w_rows = rank * rank // n_col
    p_rows = 4 * rank // n_col
    n_chip = n_col // 2
    t_rows = -(-(w_rows + p_rows) // 16) * 16
    dma = lambda n: pltpu.SemaphoreType.DMA((n,))
    vmem = pltpu.VMEM
    scratch = [
        vmem((n_res, n_sel, width), F32),
        vmem((n_res, n_sel, 1), F32),
        vmem((n_res, n_sel, width), BF),
        vmem(((n_i + 2) * n_j, k_width), F32),
        vmem((n_j, lanes, k_width), BF),
        vmem((rank, n_j * rank, lanes), BF),
        vmem((rank, n_j * rank, lanes), BF),
        vmem((n_col, chunk, n_sel), BF),
        vmem((chunk, n_sel), BF),
        vmem((n_row, chunk, n_sel), BF),
        vmem((rank * lanes, n_sel), F32),
        vmem((rank * lanes, n_sel), BF),
        vmem((n_sel, n_j * rank), BF),
        vmem((rank * lanes, n_sel), F32),
        vmem((2, n_chip, chunk, n_sel), BF),
        *[vmem((n_chip, chunk, n_sel), BF)] * 3,
        *[vmem((n_row, chunk, n_sel), BF)] * 2,
        vmem((n_col, w_rows, k_width), F32),
        vmem((n_col, t_rows, k_width), BF),
        *[vmem((n_chip, t_rows, k_width), BF)] * 3,
        vmem((t_rows, k_width), BF),
        vmem((n_row, t_rows, k_width), BF),
        *[dma(n) for n in (n_chip, n_chip, n_chip, n_chip, n_row, n_row)],
        *[dma(n) for n in (n_chip, n_chip, n_row, n_row)],
        *[dma(n) for n in (n_chip, n_chip, n_row, n_row, n_chip, n_chip, 6)],
    ]
    whole = pl.BlockSpec(memory_space=pltpu.VMEM)
    shift = jnp.concatenate([first_factor_shift, second_factor_shift]).reshape(2 * rank, 1)
    slope, sums = pl.pallas_call(
        kernel,
        out_shape=(
            jax.ShapeDtypeStruct((n_res, n_sel, width), BF),
            jax.ShapeDtypeStruct((n_col, t_rows, k_width), BF),
        ),
        in_specs=[whole] * 9,
        out_specs=(whole,) * 2,
        scratch_shapes=scratch,
        compiler_params=pltpu.CompilerParams(
            collective_id=0, has_side_effects=True, vmem_limit_bytes=60 * 1024 * 1024
        ),
    )(
        alignment_embedding.transpose(1, 0, 2),
        chosen_sequence_ids.reshape(1, n_sel),
        standardizer_scale.reshape(1, width),
        standardizer_offset.reshape(1, width),
        first_factor_matrix.T,
        second_factor_matrix.T,
        shift,
        final_matrix,
        twosite_delta_cotangent,
    )
    slope, grad_a, grad_b, grad_w = pl.pallas_call(
        last_kernel,
        out_shape=(
            jax.ShapeDtypeStruct((n_res, n_sel, width), BF),
            jax.ShapeDtypeStruct((rank, width), F32),
            jax.ShapeDtypeStruct((rank, width), F32),
            jax.ShapeDtypeStruct((rank * rank, k_width), F32),
        ),
        in_specs=[whole] * 2,
        out_specs=(whole,) * 4,
    )(slope, sums)
    return slope.transpose(1, 0, 2), grad_a.T, grad_b.T, grad_w


def solution(mesh):
    return jax.shard_map(
        functools.partial(shards, mesh.shape["row"], mesh.shape["col"]),
        mesh=mesh,
        in_specs=(
            P(None, ("row", "col"), None),
            P(),
            P(),
            P(),
            P(),
            P(),
            P(),
            P(),
            P(),
            P("row", "col", None),
        ),
        out_specs=(P(None, ("row", "col"), None), P(), P(), P()),
        check_vma=False,
    )
```

```python
import functools

import jax
import jax.numpy as jnp
from jax import lax
from jax.experimental import pallas as pl
from jax.experimental.pallas import tpu as pltpu
from jax.sharding import PartitionSpec as P

CHOSEN_SEQUENCES = 128
SLOT = 8

BF = jnp.bfloat16
F32 = jnp.float32
NN = (((1,), (0,)), ((), ()))
NT = (((1,), (1,)), ((), ()))


def dot(left, right, dims=NN):
    return lax.dot_general(left, right, dims, preferred_element_type=F32)


def kernel(
    emb_hbm, ids_ref, scale_ref, offset_ref, w_a_ref, w_b_ref, shift_ref, final_hbm, dz_hbm,
    slope_ref, sums_ref,
    emb_ref, final_ref, dz_ref, in_sems, xhat_ref, inv_ref, normed_ref, dzf_ref, dzb_ref, d_ref, o_ref,
    abuf, bsend, bbuf, atf_ref, at_ref, bt_ref, daf_ref, sa, ra0, sa1, ra1, sb, rb, d_sum, d_own, wacc_ref,
    st0, rt0, st1, rt1,
    ssem_a, rsem_a, ssem_a2, rsem_a2, ssem_b, rsem_b, ssem_ra, rsem_ra, ssem_rb, rsem_rb,
    t_sems, sib_sems,
):
    n_row, n_col = bbuf.shape[0], abuf.shape[0]
    n_chip = n_col // 2
    n_res, n_sel, width = normed_ref.shape
    rank = w_a_ref.shape[0]
    n_j = n_row * n_res
    lanes = n_col * SLOT
    chunk = n_res * rank
    row, col = lax.axis_index("row"), lax.axis_index("col")
    me = row * n_col + col
    b_col, b_slot = me // n_row, me % n_row
    chip, core = col // 2, col % 2
    other = 1 - core
    sibling = (row, col + 1 - 2 * core)

    def copy(src, dst, send_sem, recv_sem, device):
        return pltpu.make_async_remote_copy(
            src_ref=src, dst_ref=dst, send_sem=send_sem, recv_sem=recv_sem,
            device_id=device, device_id_type=pl.DeviceIdType.MESH,
        )

    def each(count, body):
        lax.fori_loop(0, count, lambda i, _: (body(i), None)[1], None)

    def chip_peer(t):
        return lax.rem(chip + t, n_chip)

    def at_chip(q):
        return (row, 2 * q + core)

    n_ring = n_row * n_chip
    ring = row * n_chip + chip

    def at_ring(u):
        return (u // n_chip, 2 * (u % n_chip) + core)

    def each_ring(body):
        half = n_ring // 2
        each(half, lambda t: body(lax.rem(ring + half + t, n_ring)))
        each(half - 1, lambda t: body(lax.rem(ring + 1 + t, n_ring)))

    def row_peer(t):
        return lax.rem(row + t, n_row)

    owner = ((n_row * col + row) // n_col, (n_row * col + row) % n_col)
    taker = (b_slot, b_col)
    stays = jnp.logical_and(b_slot == row, b_col == col)

    loads = [
        pltpu.make_async_copy(src, dst, in_sems.at[i])
        for i, (src, dst) in enumerate(
            [(emb_hbm, emb_ref), (dz_hbm, dz_ref), (final_hbm, final_ref)]
        )
    ]
    for load in loads:
        load.start()

    barrier = pltpu.get_barrier_semaphore()

    def greet(device):
        pl.semaphore_signal(barrier, inc=1, device_id=device, device_id_type=pl.DeviceIdType.MESH)

    greet(sibling)
    each_ring(lambda u: greet(at_ring(u)))

    @pl.when(jnp.logical_not(stays))
    def _():
        greet(owner)
        greet(taker)

    n_all = emb_ref.shape[1]
    ids = jnp.broadcast_to(ids_ref[...], (n_sel, n_sel)).T
    ids = jnp.concatenate([ids] * (n_all // n_sel), axis=1)
    picks = (lax.broadcasted_iota(jnp.int32, (n_sel, n_all), 1) == ids).astype(F32).astype(BF)
    loads[0].wait()
    w_both = jnp.concatenate([w_a_ref[...], w_b_ref[...]], axis=0)
    for r in range(n_res):
        x = dot(picks, emb_ref[r])
        centred = x - jnp.mean(x, axis=-1, keepdims=True)
        inverse = lax.rsqrt(jnp.mean(centred * centred, axis=-1, keepdims=True) + 1e-05)
        xhat = centred * inverse
        xhat_ref[r] = xhat
        inv_ref[r] = inverse
        normed = (xhat * scale_ref[...] + offset_ref[...]).astype(BF)
        normed_ref[r] = normed
        proj = (dot(w_both, normed, NT) + shift_ref[...]).astype(BF)
        abuf[col, r * rank : (r + 1) * rank, :] = proj[:rank]
        bsend[r * rank : (r + 1) * rank, :] = proj[rank:]

    loads[1].wait()
    loads[2].wait()
    n_i, j_width, k_width = dz_ref.shape
    dzf_ref[pl.ds(0, n_i * j_width), :] = dz_ref[...].astype(F32).reshape(n_i * j_width, k_width)
    dzf_ref[pl.ds(n_i * j_width, 2 * j_width), :] = jnp.zeros((2 * j_width, k_width), F32)
    atf_ref[...] = jnp.zeros(atf_ref.shape, F32)

    def spread(j):
        rows = [
            dzf_ref[pl.ds(n_res * q * j_width + j, SLOT, stride=j_width), :] for q in range(n_col)
        ]
        dzb_ref[j] = jnp.concatenate(rows, axis=0).astype(BF)

    each(n_j, spread)

    pl.semaphore_wait(barrier, n_ring + jnp.where(stays, 0, 2))

    first_b = copy(bsend, bbuf.at[b_slot], sib_sems.at[6], sib_sems.at[7], taker)

    @pl.when(stays)
    def _():
        bbuf[b_slot] = bsend[...]

    @pl.when(jnp.logical_not(stays))
    def _():
        first_b.start()

    def b_copy(t, q):
        return copy(bbuf.at[row], bbuf.at[row], ssem_b.at[t], rsem_b.at[row], (q, col))

    def a_copy(t, q):
        return copy(abuf.at[col], abuf.at[col], ssem_a.at[t], rsem_a.at[chip], at_chip(q))

    def a_forward(q):
        block = abuf.at[2 * q + core]
        return copy(block, block, ssem_a2.at[q], rsem_a2.at[q], sibling)

    each(n_chip - 1, lambda t: a_copy(t, chip_peer(t + 1)).start())
    a_forward(chip).start()

    @pl.when(jnp.logical_not(stays))
    def _():
        copy(bsend, bbuf.at[row], sib_sems.at[6], sib_sems.at[7], owner).wait_recv()

    each(n_row - 1, lambda t: b_copy(t, row_peer(t + 1)).start())

    def d_step(step):
        pair = dzb_ref[pl.ds(2 * step, 2)].reshape(2 * lanes, k_width)
        d = dot(final_ref[...], pair, NT).astype(BF)
        for q in range(2):
            at = pl.ds(pl.multiple_of((2 * step + q) * rank, rank), rank)
            d_ref[:, at, :] = d[:, q * lanes : (q + 1) * lanes].reshape(rank, rank, lanes)

    each(n_j // 2, d_step)

    def wait_b(t):
        q = row_peer(n_row - 1 - t)
        copy(bbuf.at[q], bbuf.at[q], ssem_b.at[t], rsem_b.at[q], (q, col)).wait_recv()

    each(n_row - 1, wait_b)
    right_t = bbuf[...].reshape(n_j * rank, n_sel)
    bt_ref[...] = right_t.T

    def part_a_step(step):
        d = jnp.concatenate([d_ref[2 * step], d_ref[2 * step + 1]], axis=1)
        part = dot(bt_ref[...], d) * (1.0 / CHOSEN_SEQUENCES)
        for q in range(2):
            at = pl.ds(pl.multiple_of((2 * step + q) * lanes, lanes), lanes)
            daf_ref[at, :] = part[:, q * lanes : (q + 1) * lanes].T

    def pass_a(t):
        q = chip_peer(n_chip - 1 - t)
        block = abuf.at[2 * q + core]
        copy(block, block, ssem_a.at[t], rsem_a.at[q], at_chip(q)).wait_recv()
        a_forward(q).start()

    each(n_chip - 1, pass_a)

    each(rank // 8, part_a_step)

    def take_a(q):
        for r in range(n_res):
            atf_ref[pl.ds(q * SLOT + r, rank, stride=lanes), :] = abuf[
                q, r * rank : (r + 1) * rank, :
            ].astype(F32)

    def wait_a(q):
        block = abuf.at[2 * q + other]
        copy(block, block, ssem_a2.at[q], rsem_a2.at[q], sibling).wait_recv()
        take_a(2 * q)
        take_a(2 * q + 1)

    each(n_chip, wait_a)

    def cast_a(c):
        at = pl.ds(pl.multiple_of(c * 4 * lanes, 4 * lanes), 4 * lanes)
        at_ref[at, :] = atf_ref[at, :].astype(BF)

    each(rank // 4, cast_a)

    def rb_copy(t, k):
        return copy(sb.at[k], rb.at[row], ssem_rb.at[t], rsem_rb.at[row], (k, col))

    def part_b_block(k):
        at = pl.ds(pl.multiple_of(k * chunk, chunk), chunk)
        total = jnp.zeros((chunk, n_sel), F32)
        for c in range(0, rank, 2):
            d = jnp.concatenate([d_ref[c, at, :], d_ref[c + 1, at, :]], axis=1)
            total += dot(d, at_ref[c * lanes : (c + 2) * lanes, :])
        return (total * (1.0 / CHOSEN_SEQUENCES)).astype(BF)

    def part_b_step(t):
        k = row_peer(t + 1)
        sb[k] = part_b_block(k)
        rb_copy(t, k).start()

    each(n_row - 1, part_b_step)
    rb[row] = part_b_block(row)

    each(rank // 2 - rank // 8, lambda step: part_a_step(rank // 8 + step))

    def pack_a(q):
        for k in range(2):
            for r in range(n_res):
                sa[k, q, r * rank : (r + 1) * rank, :] = daf_ref[
                    pl.ds((2 * q + k) * SLOT + r, rank, stride=lanes), :
                ].astype(BF)

    each(n_chip, pack_a)

    def sib_copy(i, src, dst):
        return copy(src, dst, sib_sems.at[i], sib_sems.at[i + 1], sibling)

    ra_sib = sib_copy(0, sa.at[other], ra0)
    ra_sib.start()

    def wait_rb(t):
        q = row_peer(n_row - 1 - t)
        copy(sb.at[q], rb.at[q], ssem_rb.at[t], rsem_rb.at[q], (q, col)).wait_recv()

    each(n_row - 1, wait_rb)
    d_sum[...] = jnp.sum(rb[...].astype(F32), axis=0).astype(BF)
    last_b = copy(d_sum, d_own, sib_sems.at[8], sib_sems.at[9], owner)

    @pl.when(stays)
    def _():
        d_own[...] = d_sum[...]

    @pl.when(jnp.logical_not(stays))
    def _():
        last_b.start()

    def o_step(step):
        at = pl.ds(pl.multiple_of(2 * step * lanes, 2 * lanes), 2 * lanes)
        o = dot(bbuf[...].reshape(n_j * rank, n_sel), at_ref[at, :], NT).astype(BF)
        o_ref[2 * step] = o[:, :lanes]
        o_ref[2 * step + 1] = o[:, lanes:]

    each(rank // 8, o_step)

    def ra_copy(t, q):
        return copy(sa1.at[q], ra1.at[chip], ssem_ra.at[t], rsem_ra.at[chip], at_chip(q))

    ra_sib.wait_recv()

    def send_part_a(t):
        q = chip_peer(t + 1)
        sa1[q] = (sa[core, q].astype(F32) + ra0[q].astype(F32)).astype(BF)
        ra_copy(t, q).start()

    each(n_chip - 1, send_part_a)
    ra1[chip] = (sa[core, chip].astype(F32) + ra0[chip].astype(F32)).astype(BF)

    each(rank // 2 - rank // 8, lambda step: o_step(rank // 8 + step))

    w_rows, p_rows = rank * rank // (2 * n_ring), 4 * rank // (2 * n_ring)
    wacc_ref[...] = jnp.zeros(wacc_ref.shape, F32)
    j_group = n_j // 6

    def w_step(step):
        pieces = []
        for q in range(j_group):
            at = pl.ds(pl.multiple_of((j_group * step + q) * rank, rank), rank)
            pieces.append(o_ref[:, at, :].reshape(rank * rank, lanes))
        z = dzb_ref[pl.ds(j_group * step, j_group)].reshape(j_group * lanes, k_width)
        part = dot(jnp.concatenate(pieces, axis=1), z)
        wacc_ref[...] += part.reshape(wacc_ref.shape)

    each(6, w_step)
    def wait_ra(t):
        q = chip_peer(n_chip - 1 - t)
        copy(sa1.at[q], ra1.at[q], ssem_ra.at[t], rsem_ra.at[q], at_chip(q)).wait_recv()

    each(n_chip - 1, wait_ra)

    @pl.when(jnp.logical_not(stays))
    def _():
        copy(d_sum, d_own, sib_sems.at[8], sib_sems.at[9], taker).wait_recv()

    d_a = jnp.sum(ra1[...].astype(F32), axis=0).astype(BF)
    d_b = d_own[...]
    d_both = [
        jnp.concatenate(
            [d_a[r * rank : (r + 1) * rank], d_b[r * rank : (r + 1) * rank]], axis=0
        )
        for r in range(n_res)
    ]
    part_p = jnp.zeros((2 * rank, width), F32)
    for r in range(n_res):
        part_p += dot(d_both[r], normed_ref[r])
    half = width // 2
    part_p = jnp.concatenate([part_p[:, :half], part_p[:, half:]], axis=0)

    st0[:, :w_rows, :] = (wacc_ref[...] * (1.0 / CHOSEN_SEQUENCES)).astype(BF)
    spare = jnp.zeros((2 * n_ring, st0.shape[1] - w_rows - p_rows, half), F32)
    tail = [part_p.reshape(2 * n_ring, p_rows, half), spare]
    st0[:, w_rows:, :] = jnp.concatenate(tail, axis=1).astype(BF)
    t_sib = sib_copy(2, st0.at[pl.ds(other * n_ring, n_ring)], rt0)
    t_sib.start()

    def layer_norm_back(r):
        g = lax.dot_general(
            d_both[r], w_both, (((0,), (0,)), ((), ())), preferred_element_type=F32
        )
        g = g * scale_ref[...]
        xhat = xhat_ref[r]
        slope = inv_ref[r] * (
            g
            - jnp.mean(g, axis=-1, keepdims=True)
            - xhat * jnp.mean(g * xhat, axis=-1, keepdims=True)
        )
        slope_ref[r] = slope.astype(BF)

    layer_norm_back(0)
    t_sib.wait_recv()

    mine = pl.ds(core * n_ring, n_ring)
    others = pl.ds(0, n_ring - 1)
    st1[...] = (st0[mine].astype(F32) + rt0[...].astype(F32)).astype(BF)

    def t1_copy(u, src, dst):
        return copy(src, dst, t_sems.at[0], t_sems.at[1], at_ring(u))

    each_ring(lambda u: t1_copy(u, st1.at[u], rt1.at[ring]).start())
    rt1[ring] = st1[ring]
    for r in range(1, n_res // 2):
        layer_norm_back(r)
    t1_all = t1_copy(ring, st1.at[others], rt1.at[others])
    t1_all.wait_recv()
    sums_ref[core * n_ring + ring] = jnp.sum(rt1[...].astype(F32), axis=0).astype(BF)

    def t2_copy(u, block):
        return copy(block, block, t_sems.at[2], t_sems.at[3], at_ring(u))

    each_ring(lambda u: t2_copy(u, sums_ref.at[core * n_ring + ring]).start())
    for r in range(n_res // 2, n_res):
        layer_norm_back(r)
    t2_all = t2_copy(ring, sums_ref.at[pl.ds(core * n_ring, n_ring - 1)])
    t2_all.wait_recv()
    back = sib_copy(4, sums_ref.at[mine], sums_ref.at[mine])
    theirs = sums_ref.at[pl.ds(other * n_ring, n_ring)]
    back.start()
    sib_copy(4, theirs, theirs).wait_recv()

    @pl.when(jnp.logical_not(stays))
    def _():
        first_b.wait_send()
        last_b.wait_send()

    def sent_row(t):
        q = row_peer(t + 1)
        for made in (b_copy, rb_copy):
            made(t, q).wait_send()

    each(n_row - 1, sent_row)

    def sent_chip(t):
        q = chip_peer(t + 1)
        for made in (a_copy, ra_copy):
            made(t, q).wait_send()

    each(n_chip - 1, sent_chip)
    each(n_chip, lambda q: a_forward(q).wait_send())
    ra_sib.wait_send()
    t_sib.wait_send()

    t1_all.wait_send()
    t2_all.wait_send()
    back.wait_send()


def last_kernel(slope_ref, sums_ref, out_ref, grad_a_ref, grad_b_ref, grad_w_ref):
    out_ref[...] = slope_ref[...]
    rank = grad_a_ref.shape[0]
    n = sums_ref.shape[0]
    w_rows, p_rows = rank * rank // n, 4 * rank // n
    pieces = []
    for i in range(n):
        piece = sums_ref[i].astype(F32)
        grad_w_ref[i * w_rows : (i + 1) * w_rows, :] = piece[:w_rows]
        pieces.append(piece[w_rows : w_rows + p_rows])
    both = jnp.concatenate(pieces, axis=0)
    grad_a_ref[...] = jnp.concatenate([both[:rank], both[2 * rank : 3 * rank]], axis=1)
    grad_b_ref[...] = jnp.concatenate([both[rank : 2 * rank], both[3 * rank :]], axis=1)


def shards(
    n_row,
    n_col,
    alignment_embedding,
    chosen_sequence_ids,
    standardizer_scale,
    standardizer_offset,
    first_factor_matrix,
    first_factor_shift,
    second_factor_matrix,
    second_factor_shift,
    final_matrix,
    twosite_delta_cotangent,
):
    width, rank = first_factor_matrix.shape
    n_sel = chosen_sequence_ids.shape[0]
    n_res = alignment_embedding.shape[1]
    n_i, n_j, k_width = twosite_delta_cotangent.shape
    lanes = n_col * SLOT
    chunk = n_res * rank
    n_ring = n_row * n_col // 2
    w_rows = rank * rank // (2 * n_ring)
    p_rows = 4 * rank // (2 * n_ring)
    n_chip = n_col // 2
    t_rows = -(-(w_rows + p_rows) // 16) * 16
    dma = lambda n: pltpu.SemaphoreType.DMA((n,))
    vmem = pltpu.VMEM
    scratch = [
        vmem((n_res, alignment_embedding.shape[0], width), BF),
        vmem(final_matrix.shape, BF),
        vmem(twosite_delta_cotangent.shape, BF),
        dma(3),
        vmem((n_res, n_sel, width), F32),
        vmem((n_res, n_sel, 1), F32),
        vmem((n_res, n_sel, width), BF),
        vmem(((n_i + 2) * n_j, k_width), F32),
        vmem((n_j, lanes, k_width), BF),
        vmem((rank, n_j * rank, lanes), BF),
        vmem((rank, n_j * rank, lanes), BF),
        vmem((n_col, chunk, n_sel), BF),
        vmem((chunk, n_sel), BF),
        vmem((n_row, chunk, n_sel), BF),
        vmem((rank * lanes, n_sel), F32),
        vmem((rank * lanes, n_sel), BF),
        vmem((n_sel, n_j * rank), BF),
        vmem((rank * lanes, n_sel), F32),
        vmem((2, n_chip, chunk, n_sel), BF),
        *[vmem((n_chip, chunk, n_sel), BF)] * 3,
        *[vmem((n_row, chunk, n_sel), BF)] * 2,
        *[vmem((chunk, n_sel), BF)] * 2,
        vmem((2 * n_ring, w_rows, k_width), F32),
        vmem((2 * n_ring, t_rows, k_width), BF),
        *[vmem((n_ring, t_rows, k_width), BF)] * 3,
        *[dma(n) for n in (n_chip, n_chip, n_chip, n_chip, n_row, n_row)],
        *[dma(n) for n in (n_chip, n_chip, n_row, n_row)],
        dma(4),
        dma(10),
    ]
    whole = pl.BlockSpec(memory_space=pltpu.VMEM)
    hbm = pl.BlockSpec(memory_space=pl.ANY)
    shift = jnp.concatenate([first_factor_shift, second_factor_shift]).reshape(2 * rank, 1)
    slope, sums = pl.pallas_call(
        kernel,
        out_shape=(
            jax.ShapeDtypeStruct((n_res, n_sel, width), BF),
            jax.ShapeDtypeStruct((2 * n_ring, t_rows, k_width), BF),
        ),
        in_specs=[hbm, *[whole] * 6, hbm, hbm],
        out_specs=(whole,) * 2,
        scratch_shapes=scratch,
        compiler_params=pltpu.CompilerParams(
            collective_id=0, has_side_effects=True, vmem_limit_bytes=60 * 1024 * 1024
        ),
    )(
        alignment_embedding.transpose(1, 0, 2),
        chosen_sequence_ids.reshape(1, n_sel),
        standardizer_scale.reshape(1, width),
        standardizer_offset.reshape(1, width),
        first_factor_matrix.T,
        second_factor_matrix.T,
        shift,
        final_matrix,
        twosite_delta_cotangent,
    )
    slope, grad_a, grad_b, grad_w = pl.pallas_call(
        last_kernel,
        out_shape=(
            jax.ShapeDtypeStruct((n_res, n_sel, width), BF),
            jax.ShapeDtypeStruct((rank, width), F32),
            jax.ShapeDtypeStruct((rank, width), F32),
            jax.ShapeDtypeStruct((rank * rank, k_width), F32),
        ),
        in_specs=[whole] * 2,
        out_specs=(whole,) * 4,
    )(slope, sums)
    return slope.transpose(1, 0, 2), grad_a.T, grad_b.T, grad_w


def solution(mesh):
    return jax.shard_map(
        functools.partial(shards, mesh.shape["row"], mesh.shape["col"]),
        mesh=mesh,
        in_specs=(
            P(None, ("row", "col"), None),
            P(),
            P(),
            P(),
            P(),
            P(),
            P(),
            P(),
            P(),
            P("row", "col", None),
        ),
        out_specs=(P(None, ("row", "col"), None), P(), P(), P()),
        check_vma=False,
    )
```

```python
import functools

import jax
import jax.numpy as jnp
from jax import lax
from jax.experimental import pallas as pl
from jax.experimental.pallas import tpu as pltpu
from jax.sharding import PartitionSpec as P

CHOSEN_SEQUENCES = 128
ROWS = 16
SLOT = 8

BF = jnp.bfloat16
F32 = jnp.float32
NN = (((1,), (0,)), ((), ()))
NT = (((1,), (1,)), ((), ()))


def dot(left, right, dims=NN):
    return lax.dot_general(left, right, dims, preferred_element_type=F32)


def kernel(
    emb_hbm, ids_ref, scale_ref, offset_ref, w_a_ref, w_b_ref, shift_ref, final_hbm, dz_hbm,
    slope_hbm, sums_ref,
    emb_ref, final_ref, dz_ref, slope_ref, in_sems, xhat_ref, inv_ref, normed_ref, dzf_ref, dzb_ref, d_ref, o_ref,
    abuf, bsend, bbuf, atf_ref, at_ref, bt_ref, daf_ref, sa, ra0, sa1, ra1, sb, rb, d_sum, d_own, wacc_ref,
    st0, rt0, st1, rt1,
    ssem_a, rsem_a, ssem_a2, rsem_a2, ssem_b, rsem_b, ssem_ra, rsem_ra, ssem_rb, rsem_rb,
    t_sems, sib_sems,
):
    n_row, n_col = bbuf.shape[0], abuf.shape[0]
    n_chip = n_col // 2
    n_res, n_sel, width = normed_ref.shape
    rank = w_a_ref.shape[0]
    n_j = n_row * n_res
    lanes = n_col * SLOT
    chunk = n_res * rank
    row, col = lax.axis_index("row"), lax.axis_index("col")
    me = row * n_col + col
    b_col, b_slot = me // n_row, me % n_row
    chip, core = col // 2, col % 2
    other = 1 - core
    sibling = (row, col + 1 - 2 * core)

    def copy(src, dst, send_sem, recv_sem, device):
        return pltpu.make_async_remote_copy(
            src_ref=src, dst_ref=dst, send_sem=send_sem, recv_sem=recv_sem,
            device_id=device, device_id_type=pl.DeviceIdType.MESH,
        )

    def each(count, body):
        lax.fori_loop(0, count, lambda i, _: (body(i), None)[1], None)

    def chip_peer(t):
        return lax.rem(chip + t, n_chip)

    def at_chip(q):
        return (row, 2 * q + core)

    n_ring = n_row * n_chip
    ring = row * n_chip + chip

    def at_ring(u):
        return (u // n_chip, 2 * (u % n_chip) + core)

    def each_ring(body):
        half = n_ring // 2
        each(half, lambda t: body(lax.rem(ring + half + t, n_ring)))
        each(half - 1, lambda t: body(lax.rem(ring + 1 + t, n_ring)))

    def row_peer(t):
        return lax.rem(row + t, n_row)

    owner = ((n_row * col + row) // n_col, (n_row * col + row) % n_col)
    taker = (b_slot, b_col)
    stays = jnp.logical_and(b_slot == row, b_col == col)

    loads = [
        pltpu.make_async_copy(src, dst, in_sems.at[i])
        for i, (src, dst) in enumerate(
            [(emb_hbm, emb_ref), (dz_hbm, dz_ref), (final_hbm, final_ref)]
        )
    ]
    for load in loads:
        load.start()

    barrier = pltpu.get_barrier_semaphore()

    def greet(device):
        pl.semaphore_signal(barrier, inc=1, device_id=device, device_id_type=pl.DeviceIdType.MESH)

    greet(sibling)
    each_ring(lambda u: greet(at_ring(u)))

    @pl.when(jnp.logical_not(stays))
    def _():
        greet(owner)
        greet(taker)

    n_all = emb_ref.shape[1]
    ids = jnp.broadcast_to(ids_ref[...], (n_sel, n_sel)).T
    ids = jnp.concatenate([ids] * (n_all // n_sel), axis=1)
    picks = (lax.broadcasted_iota(jnp.int32, (n_sel, n_all), 1) == ids).astype(F32).astype(BF)
    loads[0].wait()
    w_both = jnp.concatenate([w_a_ref[...], w_b_ref[...]], axis=0)
    for r in range(n_res):
        x = dot(picks, emb_ref[r])
        centred = x - jnp.mean(x, axis=-1, keepdims=True)
        inverse = lax.rsqrt(jnp.mean(centred * centred, axis=-1, keepdims=True) + 1e-05)
        xhat = centred * inverse
        xhat_ref[r] = xhat
        inv_ref[r] = inverse
        normed = (xhat * scale_ref[...] + offset_ref[...]).astype(BF)
        normed_ref[r] = normed
        proj = (dot(w_both, normed, NT) + shift_ref[...]).astype(BF)
        abuf[col, r * rank : (r + 1) * rank, :] = proj[:rank]
        bsend[r * rank : (r + 1) * rank, :] = proj[rank:]

    loads[1].wait()
    loads[2].wait()
    n_i, j_width, k_width = dz_ref.shape
    dzf_ref[pl.ds(0, n_i * j_width), :] = dz_ref[...].astype(F32).reshape(n_i * j_width, k_width)
    dzf_ref[pl.ds(n_i * j_width, 2 * j_width), :] = jnp.zeros((2 * j_width, k_width), F32)
    atf_ref[...] = jnp.zeros(atf_ref.shape, F32)

    def spread(j):
        rows = [
            dzf_ref[pl.ds(n_res * q * j_width + j, SLOT, stride=j_width), :] for q in range(n_col)
        ]
        dzb_ref[j] = jnp.concatenate(rows, axis=0).astype(BF)

    each(n_j, spread)

    pl.semaphore_wait(barrier, n_ring + jnp.where(stays, 0, 2))

    first_b = copy(bsend, bbuf.at[b_slot], sib_sems.at[8], sib_sems.at[9], taker)

    @pl.when(stays)
    def _():
        bbuf[b_slot] = bsend[...]

    @pl.when(jnp.logical_not(stays))
    def _():
        first_b.start()

    def b_copy(t, q):
        return copy(bbuf.at[row], bbuf.at[row], ssem_b.at[t], rsem_b.at[row], (q, col))

    def a_copy(t, q):
        return copy(abuf.at[col], abuf.at[col], ssem_a.at[t], rsem_a.at[chip], at_chip(q))

    def a_forward(q):
        block = abuf.at[2 * q + core]
        return copy(block, block, ssem_a2.at[q], rsem_a2.at[q], sibling)

    each(n_chip - 1, lambda t: a_copy(t, chip_peer(t + 1)).start())
    a_forward(chip).start()

    @pl.when(jnp.logical_not(stays))
    def _():
        copy(bsend, bbuf.at[row], sib_sems.at[8], sib_sems.at[9], owner).wait_recv()

    each(n_row - 1, lambda t: b_copy(t, row_peer(t + 1)).start())

    def d_step(step):
        pair = dzb_ref[pl.ds(2 * step, 2)].reshape(2 * lanes, k_width)
        d = dot(final_ref[...], pair, NT).astype(BF)
        for q in range(2):
            at = pl.ds(pl.multiple_of((2 * step + q) * rank, rank), rank)
            d_ref[:, at, :] = d[:, q * lanes : (q + 1) * lanes].reshape(rank, rank, lanes)

    each(n_j // 2, d_step)

    def wait_b(t):
        q = row_peer(n_row - 1 - t)
        copy(bbuf.at[q], bbuf.at[q], ssem_b.at[t], rsem_b.at[q], (q, col)).wait_recv()

    each(n_row - 1, wait_b)
    right_t = bbuf[...].reshape(n_j * rank, n_sel)
    bt_ref[...] = right_t.T

    def part_a_step(step):
        d = jnp.concatenate([d_ref[2 * step], d_ref[2 * step + 1]], axis=1)
        part = dot(bt_ref[...], d) * (1.0 / CHOSEN_SEQUENCES)
        for q in range(2):
            at = pl.ds(pl.multiple_of((2 * step + q) * lanes, lanes), lanes)
            daf_ref[at, :] = part[:, q * lanes : (q + 1) * lanes].T

    def pass_a(t):
        q = chip_peer(n_chip - 1 - t)
        block = abuf.at[2 * q + core]
        copy(block, block, ssem_a.at[t], rsem_a.at[q], at_chip(q)).wait_recv()
        a_forward(q).start()

    each(n_chip - 1, pass_a)

    each(rank // 8, part_a_step)

    def take_a(q):
        for r in range(n_res):
            atf_ref[pl.ds(q * SLOT + r, rank, stride=lanes), :] = abuf[
                q, r * rank : (r + 1) * rank, :
            ].astype(F32)

    def wait_a(q):
        block = abuf.at[2 * q + other]
        copy(block, block, ssem_a2.at[q], rsem_a2.at[q], sibling).wait_recv()
        take_a(2 * q)
        take_a(2 * q + 1)

    each(n_chip, wait_a)

    def cast_a(c):
        at = pl.ds(pl.multiple_of(c * 4 * lanes, 4 * lanes), 4 * lanes)
        at_ref[at, :] = atf_ref[at, :].astype(BF)

    each(rank // 4, cast_a)

    def rb_copy(t, k):
        return copy(sb.at[k], rb.at[row], ssem_rb.at[t], rsem_rb.at[row], (k, col))

    def part_b_block(k):
        at = pl.ds(pl.multiple_of(k * chunk, chunk), chunk)
        total = jnp.zeros((chunk, n_sel), F32)
        for c in range(0, rank, 2):
            d = jnp.concatenate([d_ref[c, at, :], d_ref[c + 1, at, :]], axis=1)
            total += dot(d, at_ref[c * lanes : (c + 2) * lanes, :])
        return (total * (1.0 / CHOSEN_SEQUENCES)).astype(BF)

    def part_b_step(t):
        k = row_peer(t + 1)
        sb[k] = part_b_block(k)
        rb_copy(t, k).start()

    each(n_row - 1, part_b_step)
    rb[row] = part_b_block(row)

    each(rank // 2 - rank // 8, lambda step: part_a_step(rank // 8 + step))

    def pack_a(q):
        for k in range(2):
            for r in range(n_res):
                sa[k, q, r * rank : (r + 1) * rank, :] = daf_ref[
                    pl.ds((2 * q + k) * SLOT + r, rank, stride=lanes), :
                ].astype(BF)

    each(n_chip, pack_a)

    def sib_copy(i, src, dst):
        return copy(src, dst, sib_sems.at[i], sib_sems.at[i + 1], sibling)

    ra_sib = sib_copy(0, sa.at[other], ra0)
    ra_sib.start()

    def wait_rb(t):
        q = row_peer(n_row - 1 - t)
        copy(sb.at[q], rb.at[q], ssem_rb.at[t], rsem_rb.at[q], (q, col)).wait_recv()

    each(n_row - 1, wait_rb)
    d_sum[...] = jnp.sum(rb[...].astype(F32), axis=0).astype(BF)
    last_b = copy(d_sum, d_own, sib_sems.at[10], sib_sems.at[11], owner)

    @pl.when(stays)
    def _():
        d_own[...] = d_sum[...]

    @pl.when(jnp.logical_not(stays))
    def _():
        last_b.start()

    def o_step(step):
        at = pl.ds(pl.multiple_of(2 * step * lanes, 2 * lanes), 2 * lanes)
        o = dot(bbuf[...].reshape(n_j * rank, n_sel), at_ref[at, :], NT).astype(BF)
        o_ref[2 * step] = o[:, :lanes]
        o_ref[2 * step + 1] = o[:, lanes:]

    each(rank // 8, o_step)

    def ra_copy(t, q):
        return copy(sa1.at[q], ra1.at[chip], ssem_ra.at[t], rsem_ra.at[chip], at_chip(q))

    ra_sib.wait_recv()

    def send_part_a(t):
        q = chip_peer(t + 1)
        sa1[q] = (sa[core, q].astype(F32) + ra0[q].astype(F32)).astype(BF)
        ra_copy(t, q).start()

    each(n_chip - 1, send_part_a)
    ra1[chip] = (sa[core, chip].astype(F32) + ra0[chip].astype(F32)).astype(BF)

    each(rank // 2 - rank // 8, lambda step: o_step(rank // 8 + step))

    wacc_ref[...] = jnp.zeros(wacc_ref.shape, F32)
    j_group = n_j // 3

    def w_step(step):
        pieces = []
        for q in range(j_group):
            at = pl.ds(pl.multiple_of((j_group * step + q) * rank, rank), rank)
            pieces.append(o_ref[:, at, :].reshape(rank * rank, lanes))
        z = dzb_ref[pl.ds(j_group * step, j_group)].reshape(j_group * lanes, k_width)
        part = dot(jnp.concatenate(pieces, axis=1), z)
        wacc_ref[...] += part

    each(3, w_step)
    n_w, n_p = rank * rank // 2 // ROWS, 2 * rank // ROWS
    n_piece = n_w + n_p
    w_sum = (wacc_ref[...] * (1.0 / CHOSEN_SEQUENCES)).astype(BF)
    st0[:, :n_w] = w_sum.reshape(2, n_w, ROWS, k_width)
    w_sib = sib_copy(2, st0.at[other, pl.ds(0, n_w)], rt0.at[pl.ds(0, n_w)])
    w_sib.start()

    def wait_ra(t):
        q = chip_peer(n_chip - 1 - t)
        copy(sa1.at[q], ra1.at[q], ssem_ra.at[t], rsem_ra.at[q], at_chip(q)).wait_recv()

    each(n_chip - 1, wait_ra)

    @pl.when(jnp.logical_not(stays))
    def _():
        copy(d_sum, d_own, sib_sems.at[10], sib_sems.at[11], taker).wait_recv()

    d_a = jnp.sum(ra1[...].astype(F32), axis=0).astype(BF)
    d_b = d_own[...]
    d_both = [
        jnp.concatenate(
            [d_a[r * rank : (r + 1) * rank], d_b[r * rank : (r + 1) * rank]], axis=0
        )
        for r in range(n_res)
    ]
    part_p = jnp.zeros((2 * rank, width), F32)
    for r in range(n_res):
        part_p += dot(d_both[r], normed_ref[r])
    half = width // 2
    part_p = jnp.concatenate([part_p[:, :half], part_p[:, half:]], axis=0)

    st0[:, n_w:] = part_p.astype(BF).reshape(2, n_p, ROWS, half)
    p_sib = sib_copy(6, st0.at[other, pl.ds(n_w, n_p)], rt0.at[pl.ds(n_w, n_p)])
    p_sib.start()

    def layer_norm_back(r):
        g = lax.dot_general(
            d_both[r], w_both, (((0,), (0,)), ((), ())), preferred_element_type=F32
        )
        g = g * scale_ref[...]
        xhat = xhat_ref[r]
        slope = inv_ref[r] * (
            g
            - jnp.mean(g, axis=-1, keepdims=True)
            - xhat * jnp.mean(g * xhat, axis=-1, keepdims=True)
        )
        slope_ref[r] = slope.astype(BF)

    layer_norm_back(0)
    w_sib.wait_recv()
    p_sib.wait_recv()

    w_every, p_every = n_ring // n_w, n_ring // n_p
    owns_w = lax.rem(ring, w_every) == 0
    owns_p = lax.rem(ring, p_every) == 1
    owns = jnp.logical_or(owns_w, owns_p)
    piece = jnp.where(owns_w, ring // w_every, n_w + ring // p_every)
    st1[...] = (st0[core].astype(F32) + rt0[...].astype(F32)).astype(BF)

    def t1_copy(u, src, dst):
        return copy(src, dst, t_sems.at[0], t_sems.at[1], at_ring(u))

    def send_piece(i, u):
        @pl.when(u != ring)
        def _():
            t1_copy(u, st1.at[i], rt1.at[ring]).start()

    def send_w(t):
        i = lax.rem(ring // w_every + n_w // 2 + t, n_w)
        send_piece(i, w_every * i)

    each(n_w, send_w)
    each(n_p, lambda i: send_piece(n_w + i, p_every * i + 1))

    @pl.when(owns)
    def _():
        rt1[ring] = st1[piece]

    for r in range(1, n_res // 2):
        layer_norm_back(r)
    def t2_copy(u, block):
        return copy(block, block, t_sems.at[2], t_sems.at[3], at_ring(u))

    @pl.when(owns)
    def _():
        arrived = rt1.at[pl.ds(0, n_ring - 1)]
        t1_copy(ring, arrived, arrived).wait_recv()
        sums_ref[core, piece] = jnp.sum(rt1[...].astype(F32), axis=0).astype(BF)
        each_ring(lambda u: t2_copy(u, sums_ref.at[core, piece]).start())

    for r in range(n_res // 2, n_res):
        layer_norm_back(r)
    slope_out = pltpu.make_async_copy(slope_ref, slope_hbm, in_sems.at[0])
    slope_out.start()

    @pl.when(owns)
    def _():
        t2_copy(ring, sums_ref.at[core, pl.ds(0, n_piece - 1)]).wait_recv()

    @pl.when(jnp.logical_not(owns))
    def _():
        t2_copy(ring, sums_ref.at[core, pl.ds(0, n_piece)]).wait_recv()

    back = sib_copy(4, sums_ref.at[core], sums_ref.at[core])
    back.start()
    sib_copy(4, sums_ref.at[other], sums_ref.at[other]).wait_recv()

    @pl.when(jnp.logical_not(stays))
    def _():
        first_b.wait_send()
        last_b.wait_send()

    def sent_row(t):
        q = row_peer(t + 1)
        for made in (b_copy, rb_copy):
            made(t, q).wait_send()

    each(n_row - 1, sent_row)

    def sent_chip(t):
        q = chip_peer(t + 1)
        for made in (a_copy, ra_copy):
            made(t, q).wait_send()

    each(n_chip - 1, sent_chip)
    each(n_chip, lambda q: a_forward(q).wait_send())
    ra_sib.wait_send()
    w_sib.wait_send()
    p_sib.wait_send()

    @pl.when(owns)
    def _():
        t1_copy(ring, st1.at[pl.ds(0, n_piece - 1)], st1.at[pl.ds(0, n_piece - 1)]).wait_send()
        sent = rt1.at[pl.ds(0, n_ring - 1)]
        t2_copy(ring, sent).wait_send()

    @pl.when(jnp.logical_not(owns))
    def _():
        t1_copy(ring, st1.at[pl.ds(0, n_piece)], st1.at[pl.ds(0, n_piece)]).wait_send()

    back.wait_send()
    slope_out.wait()


def last_kernel(slope_ref, sums_ref, out_ref, grad_a_ref, grad_b_ref, grad_w_ref):
    out_ref[...] = slope_ref[...]
    rank, width = grad_a_ref.shape
    half = width // 2
    n_w = rank * rank // 2 // ROWS
    sums = sums_ref[...].astype(F32)
    grad_w_ref[...] = sums[:, :n_w].reshape(grad_w_ref.shape)
    both = sums[:, n_w:].reshape(4 * rank, half)
    grad_a_ref[...] = jnp.concatenate([both[:rank], both[2 * rank : 3 * rank]], axis=1)
    grad_b_ref[...] = jnp.concatenate([both[rank : 2 * rank], both[3 * rank :]], axis=1)


def shards(
    n_row,
    n_col,
    alignment_embedding,
    chosen_sequence_ids,
    standardizer_scale,
    standardizer_offset,
    first_factor_matrix,
    first_factor_shift,
    second_factor_matrix,
    second_factor_shift,
    final_matrix,
    twosite_delta_cotangent,
):
    width, rank = first_factor_matrix.shape
    n_sel = chosen_sequence_ids.shape[0]
    n_res = alignment_embedding.shape[1]
    n_i, n_j, k_width = twosite_delta_cotangent.shape
    lanes = n_col * SLOT
    chunk = n_res * rank
    n_ring = n_row * n_col // 2
    n_chip = n_col // 2
    n_piece = rank * rank // 2 // ROWS + 2 * rank // ROWS
    dma = lambda n: pltpu.SemaphoreType.DMA((n,))
    vmem = pltpu.VMEM
    scratch = [
        vmem((n_res, alignment_embedding.shape[0], width), BF),
        vmem(final_matrix.shape, BF),
        vmem(twosite_delta_cotangent.shape, BF),
        vmem((n_res, n_sel, width), BF),
        dma(3),
        vmem((n_res, n_sel, width), F32),
        vmem((n_res, n_sel, 1), F32),
        vmem((n_res, n_sel, width), BF),
        vmem(((n_i + 2) * n_j, k_width), F32),
        vmem((n_j, lanes, k_width), BF),
        vmem((rank, n_j * rank, lanes), BF),
        vmem((rank, n_j * rank, lanes), BF),
        vmem((n_col, chunk, n_sel), BF),
        vmem((chunk, n_sel), BF),
        vmem((n_row, chunk, n_sel), BF),
        vmem((rank * lanes, n_sel), F32),
        vmem((rank * lanes, n_sel), BF),
        vmem((n_sel, n_j * rank), BF),
        vmem((rank * lanes, n_sel), F32),
        vmem((2, n_chip, chunk, n_sel), BF),
        *[vmem((n_chip, chunk, n_sel), BF)] * 3,
        *[vmem((n_row, chunk, n_sel), BF)] * 2,
        *[vmem((chunk, n_sel), BF)] * 2,
        vmem((rank * rank, k_width), F32),
        vmem((2, n_piece, ROWS, k_width), BF),
        *[vmem((n_piece, ROWS, k_width), BF)] * 2,
        vmem((n_ring, ROWS, k_width), BF),
        *[dma(n) for n in (n_chip, n_chip, n_chip, n_chip, n_row, n_row)],
        *[dma(n) for n in (n_chip, n_chip, n_row, n_row)],
        dma(4),
        dma(12),
    ]
    whole = pl.BlockSpec(memory_space=pltpu.VMEM)
    hbm = pl.BlockSpec(memory_space=pl.ANY)
    shift = jnp.concatenate([first_factor_shift, second_factor_shift]).reshape(2 * rank, 1)
    slope, sums = pl.pallas_call(
        kernel,
        out_shape=(
            jax.ShapeDtypeStruct((n_res, n_sel, width), BF),
            jax.ShapeDtypeStruct((2, n_piece, ROWS, k_width), BF),
        ),
        in_specs=[hbm, *[whole] * 6, hbm, hbm],
        out_specs=(hbm, whole),
        scratch_shapes=scratch,
        compiler_params=pltpu.CompilerParams(
            collective_id=0, has_side_effects=True, vmem_limit_bytes=60 * 1024 * 1024
        ),
    )(
        alignment_embedding.transpose(1, 0, 2),
        chosen_sequence_ids.reshape(1, n_sel),
        standardizer_scale.reshape(1, width),
        standardizer_offset.reshape(1, width),
        first_factor_matrix.T,
        second_factor_matrix.T,
        shift,
        final_matrix,
        twosite_delta_cotangent,
    )
    slope, grad_a, grad_b, grad_w = pl.pallas_call(
        last_kernel,
        out_shape=(
            jax.ShapeDtypeStruct((n_res, n_sel, width), BF),
            jax.ShapeDtypeStruct((rank, width), F32),
            jax.ShapeDtypeStruct((rank, width), F32),
            jax.ShapeDtypeStruct((rank * rank, k_width), F32),
        ),
        in_specs=[whole] * 2,
        out_specs=(whole,) * 4,
    )(slope, sums)
    return slope.transpose(1, 0, 2), grad_a.T, grad_b.T, grad_w


def solution(mesh):
    return jax.shard_map(
        functools.partial(shards, mesh.shape["row"], mesh.shape["col"]),
        mesh=mesh,
        in_specs=(
            P(None, ("row", "col"), None),
            P(),
            P(),
            P(),
            P(),
            P(),
            P(),
            P(),
            P(),
            P("row", "col", None),
        ),
        out_specs=(P(None, ("row", "col"), None), P(), P(), P()),
        check_vma=False,
    )
```

```python
import functools

import jax
import jax.numpy as jnp
from jax import lax
from jax.experimental import pallas as pl
from jax.experimental.pallas import tpu as pltpu
from jax.sharding import PartitionSpec as P

CHOSEN_SEQUENCES = 128
ROWS = 16
SLOT = 8

BF = jnp.bfloat16
F32 = jnp.float32
NN = (((1,), (0,)), ((), ()))
NT = (((1,), (1,)), ((), ()))


def dot(left, right, dims=NN):
    return lax.dot_general(left, right, dims, preferred_element_type=F32)


def kernel(
    emb_hbm, ids_ref, scale_ref, offset_ref, w_a_ref, w_b_ref, shift_ref, final_hbm, dz_hbm,
    slope_hbm, sums_ref,
    emb_ref, final_ref, dz_ref, slope_ref, in_sems, xhat_ref, inv_ref, normed_ref, dzf_ref, dzb_ref, d_ref, o_ref,
    abuf, bsend, bbuf, atf_ref, at_ref, bt_ref, daf_ref, sa, ra0, sa1, ra1, sb, rb, d_sum, d_own, wacc_ref,
    st0, rt0, st1, rt1,
    ssem_a, rsem_a, ssem_a2, rsem_a2, ssem_b, rsem_b, ssem_ra, rsem_ra, ssem_rb, rsem_rb,
    t_sems, sib_sems,
):
    n_row, n_col = bbuf.shape[0], abuf.shape[0]
    n_chip = n_col // 2
    n_res, n_sel, width = normed_ref.shape
    rank = w_a_ref.shape[0]
    n_j = n_row * n_res
    lanes = n_col * SLOT
    chunk = n_res * rank
    row, col = lax.axis_index("row"), lax.axis_index("col")
    me = row * n_col + col
    b_col, b_slot = me // n_row, me % n_row
    chip, core = col // 2, col % 2
    other = 1 - core
    sibling = (row, col + 1 - 2 * core)

    def copy(src, dst, send_sem, recv_sem, device):
        return pltpu.make_async_remote_copy(
            src_ref=src, dst_ref=dst, send_sem=send_sem, recv_sem=recv_sem,
            device_id=device, device_id_type=pl.DeviceIdType.MESH,
        )

    def each(count, body):
        lax.fori_loop(0, count, lambda i, _: (body(i), None)[1], None)

    def each_by(size, first, count, body):
        while count % size:
            size -= 1

        def several(i):
            for k in range(size):
                body(first + size * i + k)

        each(count // size, several)

    def chip_peer(t):
        return lax.rem(chip + t, n_chip)

    def at_chip(q):
        return (row, 2 * q + core)

    n_ring = n_row * n_chip
    ring = row * n_chip + chip

    def at_ring(u):
        return (u // n_chip, 2 * (u % n_chip) + core)

    def each_ring(body):
        half = n_ring // 2
        each(half, lambda t: body(lax.rem(ring + half + t, n_ring)))
        each(half - 1, lambda t: body(lax.rem(ring + 1 + t, n_ring)))

    def row_peer(t):
        return lax.rem(row + t, n_row)

    owner = ((n_row * col + row) // n_col, (n_row * col + row) % n_col)
    taker = (b_slot, b_col)
    stays = jnp.logical_and(b_slot == row, b_col == col)

    loads = [
        pltpu.make_async_copy(src, dst, in_sems.at[i])
        for i, (src, dst) in enumerate(
            [(emb_hbm, emb_ref), (dz_hbm, dz_ref), (final_hbm, final_ref)]
        )
    ]
    for load in loads:
        load.start()

    barrier = pltpu.get_barrier_semaphore()

    def greet(device):
        pl.semaphore_signal(barrier, inc=1, device_id=device, device_id_type=pl.DeviceIdType.MESH)

    greet(sibling)
    each_ring(lambda u: greet(at_ring(u)))

    @pl.when(jnp.logical_not(stays))
    def _():
        greet(owner)
        greet(taker)

    n_all = emb_ref.shape[1]
    ids = jnp.broadcast_to(ids_ref[...], (n_sel, n_sel)).T
    ids = jnp.concatenate([ids] * (n_all // n_sel), axis=1)
    picks = (lax.broadcasted_iota(jnp.int32, (n_sel, n_all), 1) == ids).astype(F32).astype(BF)
    loads[0].wait()
    w_both = jnp.concatenate([w_a_ref[...], w_b_ref[...]], axis=0)
    for r in range(n_res):
        x = dot(picks, emb_ref[r])
        centred = x - jnp.mean(x, axis=-1, keepdims=True)
        inverse = lax.rsqrt(jnp.mean(centred * centred, axis=-1, keepdims=True) + 1e-05)
        xhat = centred * inverse
        xhat_ref[r] = xhat
        inv_ref[r] = inverse
        normed = (xhat * scale_ref[...] + offset_ref[...]).astype(BF)
        normed_ref[r] = normed
        proj = (dot(w_both, normed, NT) + shift_ref[...]).astype(BF)
        abuf[col, r * rank : (r + 1) * rank, :] = proj[:rank]
        bsend[r * rank : (r + 1) * rank, :] = proj[rank:]

    loads[1].wait()
    loads[2].wait()
    n_i, j_width, k_width = dz_ref.shape
    dzf_ref[pl.ds(0, n_i * j_width), :] = dz_ref[...].astype(F32).reshape(n_i * j_width, k_width)
    dzf_ref[pl.ds(n_i * j_width, 2 * j_width), :] = jnp.zeros((2 * j_width, k_width), F32)
    atf_ref[...] = jnp.zeros(atf_ref.shape, F32)

    def spread(j):
        rows = [
            dzf_ref[pl.ds(n_res * q * j_width + j, SLOT, stride=j_width), :] for q in range(n_col)
        ]
        dzb_ref[j] = jnp.concatenate(rows, axis=0).astype(BF)

    each_by(4, 0, n_j, spread)

    pl.semaphore_wait(barrier, n_ring + jnp.where(stays, 0, 2))

    first_b = copy(bsend, bbuf.at[b_slot], sib_sems.at[8], sib_sems.at[9], taker)

    @pl.when(stays)
    def _():
        bbuf[b_slot] = bsend[...]

    @pl.when(jnp.logical_not(stays))
    def _():
        first_b.start()

    def b_copy(t, q):
        return copy(bbuf.at[row], bbuf.at[row], ssem_b.at[t], rsem_b.at[row], (q, col))

    def a_copy(t, q):
        return copy(abuf.at[col], abuf.at[col], ssem_a.at[t], rsem_a.at[chip], at_chip(q))

    def a_forward(q):
        block = abuf.at[2 * q + core]
        return copy(block, block, ssem_a2.at[q], rsem_a2.at[q], sibling)

    each(n_chip - 1, lambda t: a_copy(t, chip_peer(t + 1)).start())
    a_forward(chip).start()

    @pl.when(jnp.logical_not(stays))
    def _():
        copy(bsend, bbuf.at[row], sib_sems.at[8], sib_sems.at[9], owner).wait_recv()

    each(n_row - 1, lambda t: b_copy(t, row_peer(t + 1)).start())

    def d_step(step):
        pair = dzb_ref[pl.ds(2 * step, 2)].reshape(2 * lanes, k_width)
        d = dot(final_ref[...], pair, NT).astype(BF)
        for q in range(2):
            at = pl.ds(pl.multiple_of((2 * step + q) * rank, rank), rank)
            d_ref[:, at, :] = d[:, q * lanes : (q + 1) * lanes].reshape(rank, rank, lanes)

    each_by(4, 0, n_j // 2, d_step)

    def wait_b(t):
        q = row_peer(n_row - 1 - t)
        copy(bbuf.at[q], bbuf.at[q], ssem_b.at[t], rsem_b.at[q], (q, col)).wait_recv()

    each(n_row - 1, wait_b)
    right_t = bbuf[...].reshape(n_j * rank, n_sel)
    bt_ref[...] = right_t.T

    def part_a_step(step):
        d = jnp.concatenate([d_ref[2 * step], d_ref[2 * step + 1]], axis=1)
        part = dot(bt_ref[...], d) * (1.0 / CHOSEN_SEQUENCES)
        for q in range(2):
            at = pl.ds(pl.multiple_of((2 * step + q) * lanes, lanes), lanes)
            daf_ref[at, :] = part[:, q * lanes : (q + 1) * lanes].T

    def pass_a(t):
        q = chip_peer(n_chip - 1 - t)
        block = abuf.at[2 * q + core]
        copy(block, block, ssem_a.at[t], rsem_a.at[q], at_chip(q)).wait_recv()
        a_forward(q).start()

    each(n_chip - 1, pass_a)

    each_by(4, 0, rank // 8, part_a_step)

    def take_a(q):
        for r in range(n_res):
            atf_ref[pl.ds(q * SLOT + r, rank, stride=lanes), :] = abuf[
                q, r * rank : (r + 1) * rank, :
            ].astype(F32)

    def wait_a(q):
        block = abuf.at[2 * q + other]
        copy(block, block, ssem_a2.at[q], rsem_a2.at[q], sibling).wait_recv()
        take_a(2 * q)
        take_a(2 * q + 1)

    each(n_chip, wait_a)

    def cast_a(c):
        at = pl.ds(pl.multiple_of(c * 4 * lanes, 4 * lanes), 4 * lanes)
        at_ref[at, :] = atf_ref[at, :].astype(BF)

    each(rank // 4, cast_a)

    def rb_copy(t, k):
        return copy(sb.at[k], rb.at[row], ssem_rb.at[t], rsem_rb.at[row], (k, col))

    def part_b_block(k):
        at = pl.ds(pl.multiple_of(k * chunk, chunk), chunk)
        total = jnp.zeros((chunk, n_sel), F32)
        for c in range(0, rank, 2):
            d = jnp.concatenate([d_ref[c, at, :], d_ref[c + 1, at, :]], axis=1)
            total += dot(d, at_ref[c * lanes : (c + 2) * lanes, :])
        return (total * (1.0 / CHOSEN_SEQUENCES)).astype(BF)

    def part_b_step(t):
        k = row_peer(t + 1)
        sb[k] = part_b_block(k)
        rb_copy(t, k).start()

    each_by(n_row - 1, 0, n_row - 1, part_b_step)
    rb[row] = part_b_block(row)

    each_by(12, rank // 8, rank // 2 - rank // 8, part_a_step)

    def pack_a(q):
        for k in range(2):
            for r in range(n_res):
                sa[k, q, r * rank : (r + 1) * rank, :] = daf_ref[
                    pl.ds((2 * q + k) * SLOT + r, rank, stride=lanes), :
                ].astype(BF)

    each(n_chip, pack_a)

    def sib_copy(i, src, dst):
        return copy(src, dst, sib_sems.at[i], sib_sems.at[i + 1], sibling)

    ra_sib = sib_copy(0, sa.at[other], ra0)
    ra_sib.start()

    def wait_rb(t):
        q = row_peer(n_row - 1 - t)
        copy(sb.at[q], rb.at[q], ssem_rb.at[t], rsem_rb.at[q], (q, col)).wait_recv()

    each(n_row - 1, wait_rb)
    d_sum[...] = jnp.sum(rb[...].astype(F32), axis=0).astype(BF)
    last_b = copy(d_sum, d_own, sib_sems.at[10], sib_sems.at[11], owner)

    @pl.when(stays)
    def _():
        d_own[...] = d_sum[...]

    @pl.when(jnp.logical_not(stays))
    def _():
        last_b.start()

    def o_step(step):
        at = pl.ds(pl.multiple_of(2 * step * lanes, 2 * lanes), 2 * lanes)
        o = dot(bbuf[...].reshape(n_j * rank, n_sel), at_ref[at, :], NT).astype(BF)
        o_ref[2 * step] = o[:, :lanes]
        o_ref[2 * step + 1] = o[:, lanes:]

    each_by(4, 0, rank // 8, o_step)

    def ra_copy(t, q):
        return copy(sa1.at[q], ra1.at[chip], ssem_ra.at[t], rsem_ra.at[chip], at_chip(q))

    ra_sib.wait_recv()

    def send_part_a(t):
        q = chip_peer(t + 1)
        sa1[q] = (sa[core, q].astype(F32) + ra0[q].astype(F32)).astype(BF)
        ra_copy(t, q).start()

    each(n_chip - 1, send_part_a)
    ra1[chip] = (sa[core, chip].astype(F32) + ra0[chip].astype(F32)).astype(BF)

    each_by(12, rank // 8, rank // 2 - rank // 8, o_step)

    wacc_ref[...] = jnp.zeros(wacc_ref.shape, F32)
    j_group = n_j // 3

    def w_step(step):
        pieces = []
        for q in range(j_group):
            at = pl.ds(pl.multiple_of((j_group * step + q) * rank, rank), rank)
            pieces.append(o_ref[:, at, :].reshape(rank * rank, lanes))
        z = dzb_ref[pl.ds(j_group * step, j_group)].reshape(j_group * lanes, k_width)
        part = dot(jnp.concatenate(pieces, axis=1), z)
        wacc_ref[...] += part

    each(3, w_step)
    n_w, n_p = rank * rank // 2 // ROWS, 2 * rank // ROWS
    n_piece = n_w + n_p
    w_sum = (wacc_ref[...] * (1.0 / CHOSEN_SEQUENCES)).astype(BF)
    st0[:, :n_w] = w_sum.reshape(2, n_w, ROWS, k_width)
    w_sib = sib_copy(2, st0.at[other, pl.ds(0, n_w)], rt0.at[pl.ds(0, n_w)])
    w_sib.start()

    def wait_ra(t):
        q = chip_peer(n_chip - 1 - t)
        copy(sa1.at[q], ra1.at[q], ssem_ra.at[t], rsem_ra.at[q], at_chip(q)).wait_recv()

    each(n_chip - 1, wait_ra)

    @pl.when(jnp.logical_not(stays))
    def _():
        copy(d_sum, d_own, sib_sems.at[10], sib_sems.at[11], taker).wait_recv()

    d_a = jnp.sum(ra1[...].astype(F32), axis=0).astype(BF)
    d_b = d_own[...]
    d_both = [
        jnp.concatenate(
            [d_a[r * rank : (r + 1) * rank], d_b[r * rank : (r + 1) * rank]], axis=0
        )
        for r in range(n_res)
    ]
    part_p = jnp.zeros((2 * rank, width), F32)
    for r in range(n_res):
        part_p += dot(d_both[r], normed_ref[r])
    half = width // 2
    part_p = jnp.concatenate([part_p[:, :half], part_p[:, half:]], axis=0)

    st0[:, n_w:] = part_p.astype(BF).reshape(2, n_p, ROWS, half)
    p_sib = sib_copy(6, st0.at[other, pl.ds(n_w, n_p)], rt0.at[pl.ds(n_w, n_p)])
    p_sib.start()

    def layer_norm_back(r):
        g = lax.dot_general(
            d_both[r], w_both, (((0,), (0,)), ((), ())), preferred_element_type=F32
        )
        g = g * scale_ref[...]
        xhat = xhat_ref[r]
        slope = inv_ref[r] * (
            g
            - jnp.mean(g, axis=-1, keepdims=True)
            - xhat * jnp.mean(g * xhat, axis=-1, keepdims=True)
        )
        slope_ref[r] = slope.astype(BF)

    layer_norm_back(0)
    w_sib.wait_recv()
    p_sib.wait_recv()

    w_every, p_every = n_ring // n_w, n_ring // n_p
    owns_w = lax.rem(ring, w_every) == 0
    owns_p = lax.rem(ring, p_every) == 1
    owns = jnp.logical_or(owns_w, owns_p)
    piece = jnp.where(owns_w, ring // w_every, n_w + ring // p_every)
    st1[...] = (st0[core].astype(F32) + rt0[...].astype(F32)).astype(BF)

    def t1_copy(u, src, dst):
        return copy(src, dst, t_sems.at[0], t_sems.at[1], at_ring(u))

    def send_piece(i, u):
        @pl.when(u != ring)
        def _():
            t1_copy(u, st1.at[i], rt1.at[ring]).start()

    def send_w(t):
        i = lax.rem(ring // w_every + n_w // 2 + t, n_w)
        send_piece(i, w_every * i)

    each(n_w, send_w)
    each(n_p, lambda i: send_piece(n_w + i, p_every * i + 1))

    @pl.when(owns)
    def _():
        rt1[ring] = st1[piece]

    for r in range(1, n_res // 2):
        layer_norm_back(r)
    def t2_copy(u, block):
        return copy(block, block, t_sems.at[2], t_sems.at[3], at_ring(u))

    @pl.when(owns)
    def _():
        arrived = rt1.at[pl.ds(0, n_ring - 1)]
        t1_copy(ring, arrived, arrived).wait_recv()
        sums_ref[core, piece] = jnp.sum(rt1[...].astype(F32), axis=0).astype(BF)
        each_ring(lambda u: t2_copy(u, sums_ref.at[core, piece]).start())

    for r in range(n_res // 2, n_res):
        layer_norm_back(r)
    slope_out = pltpu.make_async_copy(slope_ref, slope_hbm, in_sems.at[0])
    slope_out.start()

    @pl.when(owns)
    def _():
        t2_copy(ring, sums_ref.at[core, pl.ds(0, n_piece - 1)]).wait_recv()

    @pl.when(jnp.logical_not(owns))
    def _():
        t2_copy(ring, sums_ref.at[core, pl.ds(0, n_piece)]).wait_recv()

    back = sib_copy(4, sums_ref.at[core], sums_ref.at[core])
    back.start()
    sib_copy(4, sums_ref.at[other], sums_ref.at[other]).wait_recv()

    @pl.when(jnp.logical_not(stays))
    def _():
        first_b.wait_send()
        last_b.wait_send()

    def sent_row(t):
        q = row_peer(t + 1)
        for made in (b_copy, rb_copy):
            made(t, q).wait_send()

    each(n_row - 1, sent_row)

    def sent_chip(t):
        q = chip_peer(t + 1)
        for made in (a_copy, ra_copy):
            made(t, q).wait_send()

    each(n_chip - 1, sent_chip)
    each(n_chip, lambda q: a_forward(q).wait_send())
    ra_sib.wait_send()
    w_sib.wait_send()
    p_sib.wait_send()

    @pl.when(owns)
    def _():
        t1_copy(ring, st1.at[pl.ds(0, n_piece - 1)], st1.at[pl.ds(0, n_piece - 1)]).wait_send()
        sent = rt1.at[pl.ds(0, n_ring - 1)]
        t2_copy(ring, sent).wait_send()

    @pl.when(jnp.logical_not(owns))
    def _():
        t1_copy(ring, st1.at[pl.ds(0, n_piece)], st1.at[pl.ds(0, n_piece)]).wait_send()

    back.wait_send()
    slope_out.wait()


def last_kernel(slope_ref, sums_ref, out_ref, grad_a_ref, grad_b_ref, grad_w_ref):
    out_ref[...] = slope_ref[...]
    rank, width = grad_a_ref.shape
    half = width // 2
    n_w = rank * rank // 2 // ROWS
    sums = sums_ref[...].astype(F32)
    grad_w_ref[...] = sums[:, :n_w].reshape(grad_w_ref.shape)
    both = sums[:, n_w:].reshape(4 * rank, half)
    grad_a_ref[...] = jnp.concatenate([both[:rank], both[2 * rank : 3 * rank]], axis=1)
    grad_b_ref[...] = jnp.concatenate([both[rank : 2 * rank], both[3 * rank :]], axis=1)


def shards(
    n_row,
    n_col,
    alignment_embedding,
    chosen_sequence_ids,
    standardizer_scale,
    standardizer_offset,
    first_factor_matrix,
    first_factor_shift,
    second_factor_matrix,
    second_factor_shift,
    final_matrix,
    twosite_delta_cotangent,
):
    width, rank = first_factor_matrix.shape
    n_sel = chosen_sequence_ids.shape[0]
    n_res = alignment_embedding.shape[1]
    n_i, n_j, k_width = twosite_delta_cotangent.shape
    lanes = n_col * SLOT
    chunk = n_res * rank
    n_ring = n_row * n_col // 2
    n_chip = n_col // 2
    n_piece = rank * rank // 2 // ROWS + 2 * rank // ROWS
    dma = lambda n: pltpu.SemaphoreType.DMA((n,))
    vmem = pltpu.VMEM
    scratch = [
        vmem((n_res, alignment_embedding.shape[0], width), BF),
        vmem(final_matrix.shape, BF),
        vmem(twosite_delta_cotangent.shape, BF),
        vmem((n_res, n_sel, width), BF),
        dma(3),
        vmem((n_res, n_sel, width), F32),
        vmem((n_res, n_sel, 1), F32),
        vmem((n_res, n_sel, width), BF),
        vmem(((n_i + 2) * n_j, k_width), F32),
        vmem((n_j, lanes, k_width), BF),
        vmem((rank, n_j * rank, lanes), BF),
        vmem((rank, n_j * rank, lanes), BF),
        vmem((n_col, chunk, n_sel), BF),
        vmem((chunk, n_sel), BF),
        vmem((n_row, chunk, n_sel), BF),
        vmem((rank * lanes, n_sel), F32),
        vmem((rank * lanes, n_sel), BF),
        vmem((n_sel, n_j * rank), BF),
        vmem((rank * lanes, n_sel), F32),
        vmem((2, n_chip, chunk, n_sel), BF),
        *[vmem((n_chip, chunk, n_sel), BF)] * 3,
        *[vmem((n_row, chunk, n_sel), BF)] * 2,
        *[vmem((chunk, n_sel), BF)] * 2,
        vmem((rank * rank, k_width), F32),
        vmem((2, n_piece, ROWS, k_width), BF),
        *[vmem((n_piece, ROWS, k_width), BF)] * 2,
        vmem((n_ring, ROWS, k_width), BF),
        *[dma(n) for n in (n_chip, n_chip, n_chip, n_chip, n_row, n_row)],
        *[dma(n) for n in (n_chip, n_chip, n_row, n_row)],
        dma(4),
        dma(12),
    ]
    whole = pl.BlockSpec(memory_space=pltpu.VMEM)
    hbm = pl.BlockSpec(memory_space=pl.ANY)
    shift = jnp.concatenate([first_factor_shift, second_factor_shift]).reshape(2 * rank, 1)
    slope, sums = pl.pallas_call(
        kernel,
        out_shape=(
            jax.ShapeDtypeStruct((n_res, n_sel, width), BF),
            jax.ShapeDtypeStruct((2, n_piece, ROWS, k_width), BF),
        ),
        in_specs=[hbm, *[whole] * 6, hbm, hbm],
        out_specs=(hbm, whole),
        scratch_shapes=scratch,
        compiler_params=pltpu.CompilerParams(
            collective_id=0, has_side_effects=True, vmem_limit_bytes=60 * 1024 * 1024
        ),
    )(
        alignment_embedding.transpose(1, 0, 2),
        chosen_sequence_ids.reshape(1, n_sel),
        standardizer_scale.reshape(1, width),
        standardizer_offset.reshape(1, width),
        first_factor_matrix.T,
        second_factor_matrix.T,
        shift,
        final_matrix,
        twosite_delta_cotangent,
    )
    slope, grad_a, grad_b, grad_w = pl.pallas_call(
        last_kernel,
        out_shape=(
            jax.ShapeDtypeStruct((n_res, n_sel, width), BF),
            jax.ShapeDtypeStruct((rank, width), F32),
            jax.ShapeDtypeStruct((rank, width), F32),
            jax.ShapeDtypeStruct((rank * rank, k_width), F32),
        ),
        in_specs=[whole] * 2,
        out_specs=(whole,) * 4,
    )(slope, sums)
    return slope.transpose(1, 0, 2), grad_a.T, grad_b.T, grad_w


def solution(mesh):
    return jax.shard_map(
        functools.partial(shards, mesh.shape["row"], mesh.shape["col"]),
        mesh=mesh,
        in_specs=(
            P(None, ("row", "col"), None),
            P(),
            P(),
            P(),
            P(),
            P(),
            P(),
            P(),
            P(),
            P("row", "col", None),
        ),
        out_specs=(P(None, ("row", "col"), None), P(), P(), P()),
        check_vma=False,
    )
```

```python
import functools

import jax
import jax.numpy as jnp
from jax import lax
from jax.experimental import pallas as pl
from jax.experimental.pallas import tpu as pltpu
from jax.sharding import PartitionSpec as P

CHOSEN_SEQUENCES = 128
ROWS = 16
SLOT = 8

BF = jnp.bfloat16
F32 = jnp.float32
NN = (((1,), (0,)), ((), ()))
NT = (((1,), (1,)), ((), ()))


def dot(left, right, dims=NN):
    return lax.dot_general(left, right, dims, preferred_element_type=F32)


def kernel(
    emb_hbm, ids_ref, scale_ref, offset_ref, w_a_ref, w_b_ref, shift_ref, final_hbm, dz_hbm,
    slope_hbm, sums_ref,
    emb_ref, final_ref, dz_ref, slope_ref, in_sems, xhat_ref, inv_ref, normed_ref, dzf_ref, dzb_ref, d_ref, o_ref,
    abuf, bsend, bbuf, atf_ref, at_ref, bt_ref, daf_ref, sa, ra0, sa1, ra1, sb, rb, d_sum, d_own, wacc_ref,
    st0, rt0, st1, rt1,
    ssem_a, rsem_a, ssem_a2, rsem_a2, ssem_b, rsem_b, ssem_ra, rsem_ra, ssem_rb, rsem_rb,
    t_sems, sib_sems,
):
    n_row, n_col = bbuf.shape[0], abuf.shape[0]
    n_chip = n_col // 2
    n_res, n_sel, width = normed_ref.shape
    rank = w_a_ref.shape[0]
    n_j = n_row * n_res
    lanes = n_col * SLOT
    chunk = n_res * rank
    row, col = lax.axis_index("row"), lax.axis_index("col")
    me = row * n_col + col
    b_col, b_slot = me // n_row, me % n_row
    chip, core = col // 2, col % 2
    other = 1 - core
    sibling = (row, col + 1 - 2 * core)

    def copy(src, dst, send_sem, recv_sem, device):
        return pltpu.make_async_remote_copy(
            src_ref=src, dst_ref=dst, send_sem=send_sem, recv_sem=recv_sem,
            device_id=device, device_id_type=pl.DeviceIdType.MESH,
        )

    def each(count, body):
        lax.fori_loop(0, count, lambda i, _: (body(i), None)[1], None)

    def each_by(size, first, count, body):
        while count % size:
            size -= 1

        def several(i):
            for k in range(size):
                body(first + size * i + k)

        each(count // size, several)

    def chip_peer(t):
        return lax.rem(chip + t, n_chip)

    def at_chip(q):
        return (row, 2 * q + core)

    n_ring = n_row * n_chip
    ring = row * n_chip + chip

    def at_ring(u):
        return (u // n_chip, 2 * (u % n_chip) + core)

    def each_ring(body):
        half = n_ring // 2
        each(half, lambda t: body(lax.rem(ring + half + t, n_ring)))
        each(half - 1, lambda t: body(lax.rem(ring + 1 + t, n_ring)))

    def row_peer(t):
        return lax.rem(row + t, n_row)

    owner = ((n_row * col + row) // n_col, (n_row * col + row) % n_col)
    taker = (b_slot, b_col)
    stays = jnp.logical_and(b_slot == row, b_col == col)

    loads = [
        pltpu.make_async_copy(src, dst, in_sems.at[i])
        for i, (src, dst) in enumerate(
            [(emb_hbm, emb_ref), (dz_hbm, dz_ref), (final_hbm, final_ref)]
        )
    ]
    for load in loads:
        load.start()

    barrier = pltpu.get_barrier_semaphore()

    def greet(device):
        pl.semaphore_signal(barrier, inc=1, device_id=device, device_id_type=pl.DeviceIdType.MESH)

    greet(sibling)
    each_ring(lambda u: greet(at_ring(u)))

    @pl.when(jnp.logical_not(stays))
    def _():
        greet(owner)
        greet(taker)

    n_all = emb_ref.shape[1]
    ids = jnp.broadcast_to(ids_ref[...], (n_sel, n_sel)).T
    ids = jnp.concatenate([ids] * (n_all // n_sel), axis=1)
    picks = (lax.broadcasted_iota(jnp.int32, (n_sel, n_all), 1) == ids).astype(F32).astype(BF)
    loads[0].wait()
    w_both = jnp.concatenate([w_a_ref[...], w_b_ref[...]], axis=0)
    for r in range(n_res):
        x = dot(picks, emb_ref[r])
        centred = x - jnp.mean(x, axis=-1, keepdims=True)
        inverse = lax.rsqrt(jnp.mean(centred * centred, axis=-1, keepdims=True) + 1e-05)
        xhat = centred * inverse
        xhat_ref[r] = xhat
        inv_ref[r] = inverse
        normed = (xhat * scale_ref[...] + offset_ref[...]).astype(BF)
        normed_ref[r] = normed
        proj = (dot(w_both, normed, NT) + shift_ref[...]).astype(BF)
        abuf[col, r * rank : (r + 1) * rank, :] = proj[:rank]
        bsend[r * rank : (r + 1) * rank, :] = proj[rank:]

    loads[1].wait()
    loads[2].wait()
    n_i, j_width, k_width = dz_ref.shape
    dzf_ref[pl.ds(0, n_i * j_width), :] = dz_ref[...].astype(F32).reshape(n_i * j_width, k_width)
    dzf_ref[pl.ds(n_i * j_width, 2 * j_width), :] = jnp.zeros((2 * j_width, k_width), F32)
    atf_ref[...] = jnp.zeros(atf_ref.shape, F32)

    def spread(j):
        rows = [
            dzf_ref[pl.ds(n_res * q * j_width + j, SLOT, stride=j_width), :] for q in range(n_col)
        ]
        dzb_ref[j] = jnp.concatenate(rows, axis=0).astype(BF)

    each_by(4, 0, n_j, spread)

    pl.semaphore_wait(barrier, n_ring + jnp.where(stays, 0, 2))

    first_b = copy(bsend, bbuf.at[b_slot], sib_sems.at[8], sib_sems.at[9], taker)

    @pl.when(stays)
    def _():
        bbuf[b_slot] = bsend[...]

    @pl.when(jnp.logical_not(stays))
    def _():
        first_b.start()

    def b_copy(t, q):
        return copy(bbuf.at[row], bbuf.at[row], ssem_b.at[t], rsem_b.at[row], (q, col))

    def a_copy(t, q):
        return copy(abuf.at[col], abuf.at[col], ssem_a.at[t], rsem_a.at[chip], at_chip(q))

    def a_forward(q):
        block = abuf.at[2 * q + core]
        return copy(block, block, ssem_a2.at[q], rsem_a2.at[q], sibling)

    each(n_chip - 1, lambda t: a_copy(t, chip_peer(t + 1)).start())
    a_forward(chip).start()

    @pl.when(jnp.logical_not(stays))
    def _():
        copy(bsend, bbuf.at[row], sib_sems.at[8], sib_sems.at[9], owner).wait_recv()

    each(n_row - 1, lambda t: b_copy(t, row_peer(t + 1)).start())

    def d_step(step):
        pair = dzb_ref[pl.ds(2 * step, 2)].reshape(2 * lanes, k_width)
        d = dot(final_ref[...], pair, NT).astype(BF)
        for q in range(2):
            at = pl.ds(pl.multiple_of((2 * step + q) * rank, rank), rank)
            d_ref[:, at, :] = d[:, q * lanes : (q + 1) * lanes].reshape(rank, rank, lanes)

    each_by(4, 0, n_j // 2, d_step)

    def wait_b(t):
        q = row_peer(n_row - 1 - t)
        copy(bbuf.at[q], bbuf.at[q], ssem_b.at[t], rsem_b.at[q], (q, col)).wait_recv()

    each(n_row - 1, wait_b)
    right_t = bbuf[...].reshape(n_j * rank, n_sel)
    bt_ref[...] = right_t.T

    def part_a_step(step):
        d = jnp.concatenate([d_ref[2 * step], d_ref[2 * step + 1]], axis=1)
        part = dot(bt_ref[...], d) * (1.0 / CHOSEN_SEQUENCES)
        for q in range(2):
            at = pl.ds(pl.multiple_of((2 * step + q) * lanes, lanes), lanes)
            daf_ref[at, :] = part[:, q * lanes : (q + 1) * lanes].T

    def pass_a(t):
        q = chip_peer(n_chip - 1 - t)
        block = abuf.at[2 * q + core]
        copy(block, block, ssem_a.at[t], rsem_a.at[q], at_chip(q)).wait_recv()
        a_forward(q).start()

    each(n_chip - 1, pass_a)

    each_by(4, 0, rank // 8, part_a_step)

    def take_a(q):
        for r in range(n_res):
            atf_ref[pl.ds(q * SLOT + r, rank, stride=lanes), :] = abuf[
                q, r * rank : (r + 1) * rank, :
            ].astype(F32)

    def wait_a(q):
        block = abuf.at[2 * q + other]
        copy(block, block, ssem_a2.at[q], rsem_a2.at[q], sibling).wait_recv()
        take_a(2 * q)
        take_a(2 * q + 1)

    each(n_chip, wait_a)

    def cast_a(c):
        at = pl.ds(pl.multiple_of(c * 4 * lanes, 4 * lanes), 4 * lanes)
        at_ref[at, :] = atf_ref[at, :].astype(BF)

    each(rank // 4, cast_a)

    def rb_copy(t, k):
        return copy(sb.at[k], rb.at[row], ssem_rb.at[t], rsem_rb.at[row], (k, col))

    def part_b_block(k):
        at = pl.ds(pl.multiple_of(k * chunk, chunk), chunk)
        total = jnp.zeros((chunk, n_sel), F32)
        for c in range(0, rank, 2):
            d = jnp.concatenate([d_ref[c, at, :], d_ref[c + 1, at, :]], axis=1)
            total += dot(d, at_ref[c * lanes : (c + 2) * lanes, :])
        return (total * (1.0 / CHOSEN_SEQUENCES)).astype(BF)

    def part_b_step(t):
        k = row_peer(t + 1)
        sb[k] = part_b_block(k)
        rb_copy(t, k).start()

    each_by(n_row - 1, 0, n_row - 1, part_b_step)
    rb[row] = part_b_block(row)

    each_by(12, rank // 8, rank // 2 - rank // 8, part_a_step)

    def pack_a(q):
        for k in range(2):
            for r in range(n_res):
                sa[k, q, r * rank : (r + 1) * rank, :] = daf_ref[
                    pl.ds((2 * q + k) * SLOT + r, rank, stride=lanes), :
                ].astype(BF)

    each(n_chip, pack_a)

    def sib_copy(i, src, dst):
        return copy(src, dst, sib_sems.at[i], sib_sems.at[i + 1], sibling)

    ra_sib = sib_copy(0, sa.at[other], ra0)
    ra_sib.start()

    def ra_copy(t, q):
        return copy(sa1.at[q], ra1.at[chip], ssem_ra.at[t], rsem_ra.at[chip], at_chip(q))

    ra_sib.wait_recv()

    def send_part_a(t):
        q = chip_peer(t + 1)
        sa1[q] = (sa[core, q].astype(F32) + ra0[q].astype(F32)).astype(BF)
        ra_copy(t, q).start()

    each(n_chip - 1, send_part_a)
    ra1[chip] = (sa[core, chip].astype(F32) + ra0[chip].astype(F32)).astype(BF)

    def o_step(step):
        at = pl.ds(pl.multiple_of(2 * step * lanes, 2 * lanes), 2 * lanes)
        o = dot(bbuf[...].reshape(n_j * rank, n_sel), at_ref[at, :], NT).astype(BF)
        o_ref[2 * step] = o[:, :lanes]
        o_ref[2 * step + 1] = o[:, lanes:]

    each_by(4, 0, rank // 8, o_step)

    def wait_rb(t):
        q = row_peer(n_row - 1 - t)
        copy(sb.at[q], rb.at[q], ssem_rb.at[t], rsem_rb.at[q], (q, col)).wait_recv()

    each(n_row - 1, wait_rb)
    d_sum[...] = jnp.sum(rb[...].astype(F32), axis=0).astype(BF)
    last_b = copy(d_sum, d_own, sib_sems.at[10], sib_sems.at[11], owner)

    @pl.when(stays)
    def _():
        d_own[...] = d_sum[...]

    @pl.when(jnp.logical_not(stays))
    def _():
        last_b.start()

    each_by(12, rank // 8, rank // 2 - rank // 8, o_step)

    wacc_ref[...] = jnp.zeros(wacc_ref.shape, F32)
    j_group = n_j // 3

    def w_step(step):
        pieces = []
        for q in range(j_group):
            at = pl.ds(pl.multiple_of((j_group * step + q) * rank, rank), rank)
            pieces.append(o_ref[:, at, :].reshape(rank * rank, lanes))
        z = dzb_ref[pl.ds(j_group * step, j_group)].reshape(j_group * lanes, k_width)
        part = dot(jnp.concatenate(pieces, axis=1), z)
        wacc_ref[...] += part

    each(3, w_step)
    n_w, n_p = rank * rank // 2 // ROWS, 2 * rank // ROWS
    n_piece = n_w + n_p
    w_sum = (wacc_ref[...] * (1.0 / CHOSEN_SEQUENCES)).astype(BF)
    st0[:, :n_w] = w_sum.reshape(2, n_w, ROWS, k_width)
    w_sib = sib_copy(2, st0.at[other, pl.ds(0, n_w)], rt0.at[pl.ds(0, n_w)])
    w_sib.start()

    def wait_ra(t):
        q = chip_peer(n_chip - 1 - t)
        copy(sa1.at[q], ra1.at[q], ssem_ra.at[t], rsem_ra.at[q], at_chip(q)).wait_recv()

    each(n_chip - 1, wait_ra)

    @pl.when(jnp.logical_not(stays))
    def _():
        copy(d_sum, d_own, sib_sems.at[10], sib_sems.at[11], taker).wait_recv()

    d_a = jnp.sum(ra1[...].astype(F32), axis=0).astype(BF)
    d_b = d_own[...]
    d_both = [
        jnp.concatenate(
            [d_a[r * rank : (r + 1) * rank], d_b[r * rank : (r + 1) * rank]], axis=0
        )
        for r in range(n_res)
    ]
    part_p = jnp.zeros((2 * rank, width), F32)
    for r in range(n_res):
        part_p += dot(d_both[r], normed_ref[r])
    half = width // 2
    part_p = jnp.concatenate([part_p[:, :half], part_p[:, half:]], axis=0)

    st0[:, n_w:] = part_p.astype(BF).reshape(2, n_p, ROWS, half)
    p_sib = sib_copy(6, st0.at[other, pl.ds(n_w, n_p)], rt0.at[pl.ds(n_w, n_p)])
    p_sib.start()

    def layer_norm_back(r):
        g = lax.dot_general(
            d_both[r], w_both, (((0,), (0,)), ((), ())), preferred_element_type=F32
        )
        g = g * scale_ref[...]
        xhat = xhat_ref[r]
        slope = inv_ref[r] * (
            g
            - jnp.mean(g, axis=-1, keepdims=True)
            - xhat * jnp.mean(g * xhat, axis=-1, keepdims=True)
        )
        slope_ref[r] = slope.astype(BF)

    layer_norm_back(0)
    w_sib.wait_recv()
    p_sib.wait_recv()

    w_every, p_every = n_ring // n_w, n_ring // n_p
    owns_w = lax.rem(ring, w_every) == 0
    owns_p = lax.rem(ring, p_every) == 1
    owns = jnp.logical_or(owns_w, owns_p)
    piece = jnp.where(owns_w, ring // w_every, n_w + ring // p_every)
    st1[...] = (st0[core].astype(F32) + rt0[...].astype(F32)).astype(BF)

    def t1_copy(u, src, dst):
        return copy(src, dst, t_sems.at[0], t_sems.at[1], at_ring(u))

    def send_piece(i, u):
        @pl.when(u != ring)
        def _():
            t1_copy(u, st1.at[i], rt1.at[ring]).start()

    def send_w(t):
        i = lax.rem(ring // w_every + n_w // 2 + t, n_w)
        send_piece(i, w_every * i)

    each(n_w, send_w)
    each(n_p, lambda i: send_piece(n_w + i, p_every * i + 1))

    @pl.when(owns)
    def _():
        rt1[ring] = st1[piece]

    for r in range(1, n_res // 2):
        layer_norm_back(r)
    def t2_copy(u, block):
        return copy(block, block, t_sems.at[2], t_sems.at[3], at_ring(u))

    @pl.when(owns)
    def _():
        arrived = rt1.at[pl.ds(0, n_ring - 1)]
        t1_copy(ring, arrived, arrived).wait_recv()
        sums_ref[core, piece] = jnp.sum(rt1[...].astype(F32), axis=0).astype(BF)
        each_ring(lambda u: t2_copy(u, sums_ref.at[core, piece]).start())

    for r in range(n_res // 2, n_res):
        layer_norm_back(r)
    slope_out = pltpu.make_async_copy(slope_ref, slope_hbm, in_sems.at[0])
    slope_out.start()

    @pl.when(owns)
    def _():
        t2_copy(ring, sums_ref.at[core, pl.ds(0, n_piece - 1)]).wait_recv()

    @pl.when(jnp.logical_not(owns))
    def _():
        t2_copy(ring, sums_ref.at[core, pl.ds(0, n_piece)]).wait_recv()

    back = sib_copy(4, sums_ref.at[core], sums_ref.at[core])
    back.start()
    sib_copy(4, sums_ref.at[other], sums_ref.at[other]).wait_recv()

    @pl.when(jnp.logical_not(stays))
    def _():
        first_b.wait_send()
        last_b.wait_send()

    def sent_row(t):
        q = row_peer(t + 1)
        for made in (b_copy, rb_copy):
            made(t, q).wait_send()

    each(n_row - 1, sent_row)

    def sent_chip(t):
        q = chip_peer(t + 1)
        for made in (a_copy, ra_copy):
            made(t, q).wait_send()

    each(n_chip - 1, sent_chip)
    each(n_chip, lambda q: a_forward(q).wait_send())
    ra_sib.wait_send()
    w_sib.wait_send()
    p_sib.wait_send()

    @pl.when(owns)
    def _():
        t1_copy(ring, st1.at[pl.ds(0, n_piece - 1)], st1.at[pl.ds(0, n_piece - 1)]).wait_send()
        sent = rt1.at[pl.ds(0, n_ring - 1)]
        t2_copy(ring, sent).wait_send()

    @pl.when(jnp.logical_not(owns))
    def _():
        t1_copy(ring, st1.at[pl.ds(0, n_piece)], st1.at[pl.ds(0, n_piece)]).wait_send()

    back.wait_send()
    slope_out.wait()


def last_kernel(slope_ref, sums_ref, out_ref, grad_a_ref, grad_b_ref, grad_w_ref):
    out_ref[...] = slope_ref[...]
    rank, width = grad_a_ref.shape
    half = width // 2
    n_w = rank * rank // 2 // ROWS
    sums = sums_ref[...].astype(F32)
    grad_w_ref[...] = sums[:, :n_w].reshape(grad_w_ref.shape)
    both = sums[:, n_w:].reshape(4 * rank, half)
    grad_a_ref[...] = jnp.concatenate([both[:rank], both[2 * rank : 3 * rank]], axis=1)
    grad_b_ref[...] = jnp.concatenate([both[rank : 2 * rank], both[3 * rank :]], axis=1)


def shards(
    n_row,
    n_col,
    alignment_embedding,
    chosen_sequence_ids,
    standardizer_scale,
    standardizer_offset,
    first_factor_matrix,
    first_factor_shift,
    second_factor_matrix,
    second_factor_shift,
    final_matrix,
    twosite_delta_cotangent,
):
    width, rank = first_factor_matrix.shape
    n_sel = chosen_sequence_ids.shape[0]
    n_res = alignment_embedding.shape[1]
    n_i, n_j, k_width = twosite_delta_cotangent.shape
    lanes = n_col * SLOT
    chunk = n_res * rank
    n_ring = n_row * n_col // 2
    n_chip = n_col // 2
    n_piece = rank * rank // 2 // ROWS + 2 * rank // ROWS
    dma = lambda n: pltpu.SemaphoreType.DMA((n,))
    vmem = pltpu.VMEM
    scratch = [
        vmem((n_res, alignment_embedding.shape[0], width), BF),
        vmem(final_matrix.shape, BF),
        vmem(twosite_delta_cotangent.shape, BF),
        vmem((n_res, n_sel, width), BF),
        dma(3),
        vmem((n_res, n_sel, width), F32),
        vmem((n_res, n_sel, 1), F32),
        vmem((n_res, n_sel, width), BF),
        vmem(((n_i + 2) * n_j, k_width), F32),
        vmem((n_j, lanes, k_width), BF),
        vmem((rank, n_j * rank, lanes), BF),
        vmem((rank, n_j * rank, lanes), BF),
        vmem((n_col, chunk, n_sel), BF),
        vmem((chunk, n_sel), BF),
        vmem((n_row, chunk, n_sel), BF),
        vmem((rank * lanes, n_sel), F32),
        vmem((rank * lanes, n_sel), BF),
        vmem((n_sel, n_j * rank), BF),
        vmem((rank * lanes, n_sel), F32),
        vmem((2, n_chip, chunk, n_sel), BF),
        *[vmem((n_chip, chunk, n_sel), BF)] * 3,
        *[vmem((n_row, chunk, n_sel), BF)] * 2,
        *[vmem((chunk, n_sel), BF)] * 2,
        vmem((rank * rank, k_width), F32),
        vmem((2, n_piece, ROWS, k_width), BF),
        *[vmem((n_piece, ROWS, k_width), BF)] * 2,
        vmem((n_ring, ROWS, k_width), BF),
        *[dma(n) for n in (n_chip, n_chip, n_chip, n_chip, n_row, n_row)],
        *[dma(n) for n in (n_chip, n_chip, n_row, n_row)],
        dma(4),
        dma(12),
    ]
    whole = pl.BlockSpec(memory_space=pltpu.VMEM)
    hbm = pl.BlockSpec(memory_space=pl.ANY)
    shift = jnp.concatenate([first_factor_shift, second_factor_shift]).reshape(2 * rank, 1)
    slope, sums = pl.pallas_call(
        kernel,
        out_shape=(
            jax.ShapeDtypeStruct((n_res, n_sel, width), BF),
            jax.ShapeDtypeStruct((2, n_piece, ROWS, k_width), BF),
        ),
        in_specs=[hbm, *[whole] * 6, hbm, hbm],
        out_specs=(hbm, whole),
        scratch_shapes=scratch,
        compiler_params=pltpu.CompilerParams(
            collective_id=0, has_side_effects=True, vmem_limit_bytes=60 * 1024 * 1024
        ),
    )(
        alignment_embedding.transpose(1, 0, 2),
        chosen_sequence_ids.reshape(1, n_sel),
        standardizer_scale.reshape(1, width),
        standardizer_offset.reshape(1, width),
        first_factor_matrix.T,
        second_factor_matrix.T,
        shift,
        final_matrix,
        twosite_delta_cotangent,
    )
    slope, grad_a, grad_b, grad_w = pl.pallas_call(
        last_kernel,
        out_shape=(
            jax.ShapeDtypeStruct((n_res, n_sel, width), BF),
            jax.ShapeDtypeStruct((rank, width), F32),
            jax.ShapeDtypeStruct((rank, width), F32),
            jax.ShapeDtypeStruct((rank * rank, k_width), F32),
        ),
        in_specs=[whole] * 2,
        out_specs=(whole,) * 4,
    )(slope, sums)
    return slope.transpose(1, 0, 2), grad_a.T, grad_b.T, grad_w


def solution(mesh):
    return jax.shard_map(
        functools.partial(shards, mesh.shape["row"], mesh.shape["col"]),
        mesh=mesh,
        in_specs=(
            P(None, ("row", "col"), None),
            P(),
            P(),
            P(),
            P(),
            P(),
            P(),
            P(),
            P(),
            P("row", "col", None),
        ),
        out_specs=(P(None, ("row", "col"), None), P(), P(), P()),
        check_vma=False,
    )
```
